128 devices in a mesh: oct: 8 (over x, core), leaf: 16 (over y, z).
Axes of the slice: x: 4, y: 4, z: 4, core: 2. Of those that a mesh axis runs over, the one named last changes fastest.
Arguments:
- positions: bfloat16 [1024, 3, 512], P(('oct', 'leaf')), may hold values from 0.019897461 to 0.9765625
- charges: bfloat16 [1024, 32, 512], P(('oct', 'leaf')), may hold values from -6 to 6
- counts: int32 [1024], P(('oct', 'leaf')), may hold values from 32 to 512, as said below
- check_to_equiv: bfloat16 [64, 64], replicated, may hold values from -1.5 to 1.5
- up_child: bfloat16 [8, 64, 64], replicated, may hold values from -0.25 to 0.25
- down_child: bfloat16 [8, 64, 64], replicated, may hold values from -0.75 to 0.75
- translate: bfloat16 [343, 64, 64], replicated, may hold values from -0.0546875 to 0.0546875
Outputs:
- potential: float32 [1024, 32, 512], P(('oct', 'leaf'))
The draws below stay inside these ranges and needn't reach their ends.
Inputs may be any that keep to these rules, and one draw needn't show every extreme that they name: Leaf m's live points are slots 0 to counts[m] - 1; in every draw all 8 leaves of one aligned block of 8 leaves are full.
All inputs are finite; a program needn't handle non-finite values.
Results may differ from the reference program's by a relative error of at most 0.00055.
The reference program's roundings to bfloat16 on the way count: a program that leaves them out, or rounds other values in their place, can miss the bound.
Values may be sent and summed in bfloat16 or wider, within the bound.
No kernel may reach another device: no remote copies, remote signals or barrier semaphores. Data moves between devices by JAX's collectives and lax.ppermute only.
A program may use at most 192 MiB of HBM per device.

```python
import jax
import jax.numpy as jnp
import numpy as np
from jax import lax

C = 32
K = 64
P_SIZE = 512
TABLE = 343
LEAVES = 1024


def draw_counts(key, part):
    key = jax.random.fold_in(key, 11)
    first_key, second_key = jax.random.split(key)
    spread = jax.random.randint(first_key, (LEAVES,), P_SIZE // 4, P_SIZE + 1)
    result = spread * spread // P_SIZE
    chosen = jax.random.randint(second_key, (), 0, LEAVES // 8)
    result = jnp.where(jnp.arange(LEAVES) // 8 == chosen, P_SIZE, result)
    return result.astype(jnp.int32)


def level_of(key, dims, pieces, low, largest):
    def one(dim, blocks):
        steps = jax.random.uniform(jax.random.fold_in(jax.random.fold_in(key, 6), dim), (blocks,), jnp.float32, low / len(pieces), largest / len(pieces))
        return jnp.repeat(jnp.exp(steps), dims[dim] // blocks).reshape((-1,) + (1,) * (len(dims) - dim - 1))

    level = one(*pieces[0])
    for cut in pieces[1:]:
        level = level * one(*cut)
    return level


def bell_draw(stream_key, extent, scale, limit, shards=(), kind=jnp.bfloat16):
    drawn = scale * jax.random.normal(stream_key, extent, jnp.float32)
    if shards:
        drawn = drawn * level_of(stream_key, extent, shards, -0.22, 0.18)
    return jnp.clip(drawn, -limit, limit).astype(kind)


def setup_inputs(seed: int = 0) -> dict:
    seeds = jax.random.split(jax.random.key(seed), 8)
    positions = jnp.clip(0.019897461 + 0.95666504 * jax.random.uniform(seeds[0], (LEAVES, 3, P_SIZE), jnp.float32) ** level_of(seeds[0], (LEAVES, 3, P_SIZE), ((0, 128),), -0.2, 0.2), 0.019897461, 0.9765625).astype(jnp.bfloat16)
    charges = bell_draw(seeds[1], (LEAVES, C, P_SIZE), 1.0, 6.0, ((0, 128),))
    counts = draw_counts(jax.random.fold_in(seeds[7], 71), 0)
    check_to_equiv = bell_draw(seeds[3], (K, K), 16 ** -0.5, 1.5)
    up_child = bell_draw(seeds[4], (8, K, K), (8 * K) ** -0.5, 0.25)
    down_child = bell_draw(seeds[5], (8, K, K), K ** -0.5, 0.75)
    translate = bell_draw(seeds[6], (TABLE, K, K), (189 * K) ** -0.5, 0.0546875)
    return dict(positions=positions, charges=charges, counts=counts, check_to_equiv=check_to_equiv, up_child=up_child, down_child=down_child, translate=translate)


KERNEL_SCALE = 0.02
SOFTENING = 0.01

def kernel_of(square):
    return KERNEL_SCALE * lax.rsqrt(square + SOFTENING)

def lattice_points(number):
    side = int(number ** (1.0 / 3.0) + 0.5)
    spacing = 1.5 / (side - 1)
    i = np.arange(side ** 3)
    return np.stack([i % side * spacing - 0.25, i // side % side * spacing - 0.25, i // (side * side) * spacing - 0.25], 1).astype(np.float32)

def far_offsets():
    rows_list = []
    for oz in range(-3, 4):
        for oy in range(-3, 4):
            for ox in range(-3, 4):
                if max(abs(oz), abs(oy), abs(ox)) > 1:
                    rows_list.append((oz, oy, ox, (oz + 3) * 49 + (oy + 3) * 7 + (ox + 3)))
    return np.array(rows_list, np.int32)

def bit_counts(total):
    return [(total + 2) // 3, (total + 1) // 3, total // 3]

def split_bits(index, total):
    counts_per = bit_counts(total)
    result = []
    for j in range(3):
        coordinate = jnp.zeros_like(index)
        for k in range(counts_per[j]):
            coordinate = coordinate + index // 2 ** (3 * k + j) % 2 * 2 ** k
        result.append(coordinate)
    return result

def translate_level(grid, table, factor):
    depth_z, depth_y, depth_x = (grid.shape[0], grid.shape[1], grid.shape[2])
    padded = jnp.pad(grid.astype(jnp.float32), ((3, 3), (3, 3), (3, 3), (0, 0), (0, 0)))
    offsets = jnp.asarray(far_offsets())
    coord_z = jnp.arange(depth_z, dtype=jnp.int32)
    coord_y = jnp.arange(depth_y, dtype=jnp.int32)
    coord_x = jnp.arange(depth_x, dtype=jnp.int32)
    zero = jnp.zeros((), jnp.int32)

    def step(total, row):
        source = lax.dynamic_slice(padded, (row[0] + 3, row[1] + 3, row[2] + 3, zero, zero), grid.shape)
        near_z = jnp.abs((coord_z + row[0]) // 2 - coord_z // 2) <= 1
        near_y = jnp.abs((coord_y + row[1]) // 2 - coord_y // 2) <= 1
        near_x = jnp.abs((coord_x + row[2]) // 2 - coord_x // 2) <= 1
        within = near_z[:, None, None] & near_y[None, :, None] & near_x[None, None, :]
        operator = lax.dynamic_index_in_dim(table, row[3], 0, keepdims=False).astype(jnp.float32)
        term = jnp.einsum('zyxck,kj->zyxcj', source, operator, precision=lax.Precision.HIGHEST)
        return (total + jnp.where(within[:, :, :, None, None], term, jnp.float32(0.0)), None)
    total, _ = lax.scan(step, jnp.zeros(grid.shape, jnp.float32), offsets)
    return total * factor

def reference(positions, charges, counts, check_to_equiv, up_child, down_child, translate):
    total_bits = LEAVES.bit_length() - 1
    per_dim = bit_counts(total_bits)
    grid_x, grid_y, grid_z = (2 ** per_dim[0], 2 ** per_dim[1], 2 ** per_dim[2])
    index = jnp.arange(LEAVES, dtype=jnp.int32)
    leaf_x, leaf_y, leaf_z = split_bits(index, total_bits)
    slots = jnp.arange(P_SIZE, dtype=jnp.int32)
    live = slots[None, :] < counts[:, None]
    masked = jnp.where(live[:, None, :], charges, jnp.zeros((), jnp.bfloat16))
    corner = jnp.stack([leaf_x, leaf_y, leaf_z], 1).astype(jnp.float32)
    absolute = positions.astype(jnp.float32) + corner[:, :, None]
    pos_grid = jnp.zeros((grid_z + 2, grid_y + 2, grid_x + 2, 3, P_SIZE), jnp.float32)
    pos_grid = pos_grid.at[leaf_z + 1, leaf_y + 1, leaf_x + 1].set(absolute)
    charge_grid = jnp.zeros((grid_z + 2, grid_y + 2, grid_x + 2, C, P_SIZE), jnp.bfloat16)
    charge_grid = charge_grid.at[leaf_z + 1, leaf_y + 1, leaf_x + 1].set(masked)
    zero = jnp.zeros((), jnp.int32)

    def near_leaf(item):
        cz, cy, cx, target = item
        src_pos = lax.dynamic_slice(pos_grid, (cz, cy, cx, zero, zero), (3, 3, 3, 3, P_SIZE)).reshape(27, 3, P_SIZE)
        src_charge = lax.dynamic_slice(charge_grid, (cz, cy, cx, zero, zero), (3, 3, 3, C, P_SIZE)).reshape(27, C, P_SIZE)
        square = (src_pos[:, 0, :, None] - target[0][None, None, :]) ** 2
        square = square + (src_pos[:, 1, :, None] - target[1][None, None, :]) ** 2
        square = square + (src_pos[:, 2, :, None] - target[2][None, None, :]) ** 2
        kern = kernel_of(square).astype(jnp.bfloat16)
        return jnp.einsum('scp,spt->ct', src_charge.astype(jnp.float32), kern.astype(jnp.float32), precision=lax.Precision.HIGHEST)
    near = lax.map(near_leaf, (leaf_z, leaf_y, leaf_x, absolute))
    surface = jnp.asarray(lattice_points(K))
    surf_abs = corner[:, None, :] + surface[None, :, :]
    square_s = (surf_abs[:, :, 0, None] - absolute[:, 0, None, :]) ** 2
    square_s = square_s + (surf_abs[:, :, 1, None] - absolute[:, 1, None, :]) ** 2
    square_s = square_s + (surf_abs[:, :, 2, None] - absolute[:, 2, None, :]) ** 2
    shape_tab = kernel_of(square_s).astype(jnp.bfloat16)
    upward = jnp.einsum('lcp,ljp->lcj', masked.astype(jnp.float32), shape_tab.astype(jnp.float32), precision=lax.Precision.HIGHEST)
    equiv = jnp.einsum('lcj,jk->lck', upward, check_to_equiv.astype(jnp.float32), precision=lax.Precision.HIGHEST).astype(jnp.bfloat16)
    boxes = LEAVES // 8
    box_equiv = jnp.einsum('bocj,ojk->bck', equiv.reshape(boxes, 8, C, K).astype(jnp.float32), up_child.astype(jnp.float32), precision=lax.Precision.HIGHEST).astype(jnp.bfloat16)
    equiv_grid = jnp.zeros((grid_z, grid_y, grid_x, C, K), jnp.bfloat16).at[leaf_z, leaf_y, leaf_x].set(equiv)
    leaf_local = translate_level(equiv_grid, translate, 1.0)[leaf_z, leaf_y, leaf_x]
    box_x, box_y, box_z = (leaf_x[::8] // 2, leaf_y[::8] // 2, leaf_z[::8] // 2)
    box_grid = jnp.zeros((grid_z // 2, grid_y // 2, grid_x // 2, C, K), jnp.bfloat16).at[box_z, box_y, box_x].set(box_equiv)
    box_local = translate_level(box_grid, translate, 0.5)[box_z, box_y, box_x].astype(jnp.bfloat16)
    inherited = jnp.einsum('bcj,ojk->bock', box_local.astype(jnp.float32), down_child.astype(jnp.float32), precision=lax.Precision.HIGHEST).reshape(LEAVES, C, K)
    local = (inherited + leaf_local).astype(jnp.bfloat16)
    far = jnp.einsum('lck,lkp->lcp', local.astype(jnp.float32), shape_tab.astype(jnp.float32), precision=lax.Precision.HIGHEST)
    return jnp.where(live[:, None, :], near + far, jnp.float32(0.0))
```

```python
import functools

import jax
import jax.numpy as jnp
from jax import lax
from jax.experimental import pallas as pl
from jax.experimental.pallas import tpu as pltpu
from jax.sharding import PartitionSpec as P

AXES = ("oct", "leaf")
KERNEL_SCALE = 0.02
SOFTENING = 0.01
INVERSE = 1.0 / KERNEL_SCALE**2
CHUNK = 128
ROWS = 144
FEATURES = 48
MIB = 1 << 20
F32 = jnp.float32
BF16 = jnp.bfloat16
VMEM = pl.BlockSpec(memory_space=pltpu.VMEM)
SMEM = pl.BlockSpec(memory_space=pltpu.SMEM)


def bit_counts(total):
    return [(total + 2) // 3, (total + 1) // 3, total // 3]


def box_coords(index, total):
    coords = []
    for j, bits in enumerate(bit_counts(total)):
        value = 0
        for k in range(bits):
            value = value + ((index >> (3 * k + j)) & 1) * 2**k
        coords.append(value)
    return coords


def box_index(coords, total):
    index = 0
    for j, bits in enumerate(bit_counts(total)):
        for k in range(bits):
            index = index + ((coords[j] >> k) & 1) * 2 ** (3 * k + j)
    return index


def shifted(value, axis, step, total):
    pairs = []
    for device in range(2**total):
        coords = box_coords(device, total)
        coords[axis] += step
        if 0 <= coords[axis] < 2 ** bit_counts(total)[axis]:
            pairs.append((device, box_index(coords, total)))
    return lax.ppermute(value, AXES, pairs)


def pieces(x):
    first = x.astype(BF16).astype(F32)
    rest = x - first
    second = rest.astype(BF16).astype(F32)
    third = (rest - second).astype(BF16).astype(F32)
    return first, second, third


def row_index(shape):
    return lax.broadcasted_iota(jnp.int32, shape, 0)


def placed(rows, offsets):
    eight = jnp.concatenate([rows, jnp.zeros_like(rows)], 0)
    index = row_index(eight.shape)
    shift = jnp.where(index == 0, offsets[0], jnp.where(index == 1, offsets[1], offsets[2]))
    return jnp.where(index < 3, eight + shift, 0.0)


def with_rows(base, extra):
    index = row_index(base.shape)
    for k, row in enumerate(extra):
        base = jnp.where(index == 3 + k, row, base)
    return base


def source_features(rows, offsets):
    x = placed(rows, offsets)
    high = x.astype(BF16).astype(F32)
    low = x - high
    norm = INVERSE * jnp.sum(x * x, axis=0, keepdims=True)
    ones = (1.0, 1.0, 1.0)
    groups = [with_rows(high, pieces(norm)), with_rows(high, ones), high, low, low, low]
    return jnp.concatenate(groups, 0)


def target_features(rows, offsets):
    x = placed(rows, offsets)
    w1, w2, w3 = pieces((-2.0 * INVERSE) * x)
    norm = INVERSE * (jnp.sum(x * x, axis=0, keepdims=True) + SOFTENING)
    ones = (1.0, 1.0, 1.0)
    return jnp.concatenate(
        [with_rows(w1, ones), with_rows(w2, pieces(norm)), w3, w1, w2, w3], 0
    )


def pack_kernel(counts, positions, charges, low, high):
    n_points = positions.shape[2]
    n_chunks = n_points // CHUNK
    for leaf in range(8):
        out, at = (low, leaf) if leaf < 4 else (high, leaf - 4)
        count = counts[leaf]
        q = charges[leaf].astype(F32)
        slot = lax.broadcasted_iota(jnp.int32, q.shape, 1)
        q = jnp.where(slot < count, q, 0.0).astype(BF16)
        live = lax.shift_right_logical(count + (CHUNK - 1), 7).astype(F32)
        p = positions[leaf].astype(F32)
        rows = []
        for j in range(n_chunks):
            out[at, 32 * j : 32 * j + 32, :] = q[:, CHUNK * j : CHUNK * (j + 1)]
            rows.append(p[:, CHUNK * j : CHUNK * (j + 1)])
            rows.append(jnp.full((1, CHUNK), live, F32))
        out[at, 128:144, :] = jnp.concatenate(rows, 0).astype(BF16)


def upward_kernel(low, high, positions, to_equiv, targets, shape_out, equiv_out):
    n_points = positions.shape[2]
    n_chunks = n_points // CHUNK
    index = lax.broadcasted_iota(jnp.int32, (64, n_points), 0)
    surface = [
        ((index >> (2 * d)) & 3).astype(F32) * 0.5 - 0.25 for d in range(3)
    ]
    upward = []
    for leaf in range(8):
        src, at = (low, leaf) if leaf < 4 else (high, leaf - 4)
        p = positions[leaf].astype(F32)
        square = (surface[0] - p[0:1]) ** 2
        square = square + (surface[1] - p[1:2]) ** 2
        square = square + (surface[2] - p[2:3]) ** 2
        shape = (KERNEL_SCALE * lax.rsqrt(square + SOFTENING)).astype(BF16)
        shape_out[leaf] = shape
        q = jnp.concatenate([src[at, 32 * j : 32 * j + 32, :] for j in range(n_chunks)], 1)
        upward.append(
            lax.dot_general(q, shape, (((1,), (1,)), ((), ())), preferred_element_type=F32)
        )
        offsets = (leaf % 2 - 1.0, leaf // 2 % 2 - 1.0, leaf // 4 - 1.0)
        block = src[at, 128:144, :].astype(F32)
        for j in range(n_chunks):
            features = target_features(block[4 * j : 4 * j + 4], offsets)
            targets[leaf, CHUNK * j : CHUNK * (j + 1), :] = features.T.astype(BF16)
    total = jnp.concatenate(upward, 0)
    equiv = jnp.zeros(total.shape, F32)
    for piece in pieces(total)[::-1]:
        equiv = equiv + jnp.dot(piece.astype(BF16), to_equiv[...], preferred_element_type=F32)
    equiv = equiv.astype(BF16)
    equiv_out[...] = jnp.concatenate([equiv[32 * l : 32 * l + 32] for l in range(8)], 1)


def near_kernel(phase, *refs):
    if phase == "own":
        low, high, targets, out, features, live_v, live_s, queue, sem = refs
    else:
        low, high, targets, before, out, features, live_v, live_s, queue, sem = refs
    per_side = low.shape[0]
    n_targets = targets.shape[1]

    def prepare(side):
        source = (low, high)[side]

        def one(leaf, _):
            block = source[leaf, 128:144, :].astype(F32)
            if phase == "own":
                z, y, x = side + 1, (leaf >> 1) + 1, (leaf & 1) + 1
            elif phase == "z":
                z, y, x = 3 * side, (leaf >> 1) + 1, (leaf & 1) + 1
            elif phase == "x":
                z, y, x = leaf >> 1, (leaf & 1) + 1, 3 * side
            else:
                z, y, x = leaf >> 2, 3 * side, leaf & 3
            offsets = [jnp.asarray(c - 2, jnp.int32).astype(F32) for c in (x, y, z)]
            at = side * per_side + leaf
            for j in range(4):
                features[4 * at + j] = source_features(block[4 * j : 4 * j + 4], offsets).astype(
                    BF16
                )
            live_v[pl.ds(at, 1), :] = block[3:4].astype(jnp.int32)
            return 0

        lax.fori_loop(0, per_side, one, 0)

    prepare(0)
    prepare(1)
    copy = pltpu.make_async_copy(live_v, live_s, sem)
    copy.start()
    copy.wait()
    if phase == "own":
        out[...] = jnp.zeros_like(out)
    else:
        out[...] = before[...]

    def run(side, leaves, target_leaves, width):
        total = jnp.int32(0)
        for leaf in leaves:
            n_live = live_s[leaf, 0]
            for j in range(4):
                queue[total] = 4 * leaf + j
                total = total + (j < n_live).astype(jnp.int32)
        rows = jnp.concatenate([targets[t] for t in target_leaves], 0)

        def block(c, _):
            us, qs = [], []
            for k in range(width):
                at = c * width + k
                item = jnp.where(at < total, queue[jnp.minimum(at, 63)], 4 * leaves[0])
                us.append(features[item])
                leaf, part = item >> 2, pl.multiple_of((item & 3) * 32, 32)
                if side is None:
                    q = jnp.where(
                        leaf < per_side,
                        low[jnp.minimum(leaf, per_side - 1), pl.ds(part, 32), :],
                        high[jnp.maximum(leaf - per_side, 0), pl.ds(part, 32), :],
                    )
                else:
                    q = (low, high)[side][leaf - side * per_side, pl.ds(part, 32), :]
                qs.append(jnp.where(at < total, q, jnp.zeros_like(q)))
            u = jnp.concatenate(us, 1)
            q = jnp.concatenate(qs, 1)
            square = jnp.dot(rows, u, preferred_element_type=F32)
            kern = lax.rsqrt(square).astype(BF16)
            added = lax.dot_general(q, kern, (((1,), (1,)), ((), ())), preferred_element_type=F32)
            for i, t in enumerate(target_leaves):
                out[t] += added[:, n_targets * i : n_targets * (i + 1)]
            return 0

        lax.fori_loop(0, (total + width - 1) // width, block, 0)

    if phase == "own":
        def half(h, _):
            run(None, list(range(8)), [4 * h + i for i in range(4)], 4)
            return 0

        lax.fori_loop(0, 2, half, 0)
    elif phase == "z":
        for side in range(2):
            run(side, [4 * side + i for i in range(4)], [4 * side + i for i in range(4)], 4)
    elif phase == "x":
        for side in range(2):

            def part(tz, _, side=side):
                leaves = [8 * side + 2 * tz + i for i in range(6)]
                run(side, leaves, [4 * tz + side, 4 * tz + 2 + side], 4)
                return 0

            lax.fori_loop(0, 2, part, 0)
    else:
        for side in range(2):

            def part(i, _, side=side):
                tz, tx = i >> 1, i & 1
                leaves = [
                    16 * side + 4 * (tz + dz) + tx + dx for dz in range(3) for dx in range(3)
                ]
                run(side, leaves, [4 * tz + 2 * side + tx], 8)
                return 0

            lax.fori_loop(0, 4, part, 0)


def widen_kernel(table, down, wide, down_out):
    n_equiv = table.shape[2]
    window = 6 * n_equiv

    def one(i, _):
        oz, oy = i // 7 - 3, i % 7 - 3
        near = (jnp.abs(oz) <= 1) & (jnp.abs(oy) <= 1)
        rows = table[pl.ds(7 * i, 7)].astype(F32).reshape(7 * n_equiv, n_equiv)
        index = row_index(rows.shape)
        drop = near & (index >= 2 * n_equiv) & (index < 5 * n_equiv)
        rows = jnp.where(drop, 0.0, rows)
        wide[i // 7, pl.ds(pl.multiple_of((i % 7) * window, window), window), :] = jnp.concatenate(
            [rows[n_equiv:], rows[:window]], 1
        ).astype(BF16)
        return 0

    lax.fori_loop(0, 49, one, 0)
    down_out[...] = jnp.concatenate([down[l].astype(F32) for l in range(8)], 1).astype(BF16)


def far_kernel(total_bits, counts, gathered, wide, up, down, shape, near, out, boxes, region):
    n_equiv = 64
    window = 6 * n_equiv
    bits = bit_counts(total_bits)
    me = lax.axis_index("oct") * lax.axis_size("leaf") + lax.axis_index("leaf")
    cx, cy, cz = box_coords(me, total_bits)
    n_pairs = gathered.shape[0]
    zeros_up = jnp.zeros((8 * n_equiv, n_equiv), F32)
    up_rows = up[...].astype(F32).reshape(8 * n_equiv, n_equiv)
    up_even = jnp.concatenate([up_rows, zeros_up], 1).astype(BF16)
    up_odd = jnp.concatenate([zeros_up, up_rows], 1).astype(BF16)
    step = 16

    def lift(i, _):
        at = pl.ds(step * i, step)
        even = gathered[at, 0].reshape(step * 32, 8 * n_equiv)
        odd = gathered[at, 1].reshape(step * 32, 8 * n_equiv)
        both = jnp.dot(even, up_even, preferred_element_type=F32)
        both = both + jnp.dot(odd, up_odd, preferred_element_type=F32)
        boxes[at] = both.astype(BF16).reshape(step, 32, 2 * n_equiv)
        return 0

    lax.fori_loop(0, n_pairs // step, lift, 0)

    parent = cx >> 1
    total = jnp.zeros((32, 2 * n_equiv), F32)
    zero = jnp.zeros((32, 2 * n_equiv), BF16)
    span_y = 2 ** bits[1]
    for z in range(2 ** bits[2]):
        row = []
        for y in range(span_y):
            for dx in (-1, 0, 1):
                px = parent + dx
                inside = (px >= 0) & (px < 2 ** (bits[0] - 1))
                pair = box_index([2 * jnp.where(inside, px, 0), y, z], total_bits) >> 1
                row.append(jnp.where(inside, boxes[pair], zero))
        left = jnp.concatenate(row, 1)
        start = pl.multiple_of((3 - cy) * window, window)
        right = wide[z - cz + 3, pl.ds(start, span_y * window), :]
        total = total + jnp.dot(left, right, preferred_element_type=F32)
    total = 0.5 * total
    total = jnp.where((cx & 1) == 0, total, pltpu.roll(total, n_equiv, 1))
    box_local = total[:, :n_equiv].astype(BF16)
    inherited = jnp.dot(box_local, down[...], preferred_element_type=F32)

    region[0] = jnp.zeros_like(region[0])
    region[7] = jnp.zeros_like(region[7])
    for bz in range(3):
        for by in range(3):
            for bx in range(3):
                z, y, x = cz + bz - 1, cy + by - 1, cx + bx - 1
                inside = (
                    (z >= 0)
                    & (z < 2 ** bits[2])
                    & (y >= 0)
                    & (y < 2 ** bits[1])
                    & (x >= 0)
                    & (x < 2 ** bits[0])
                )
                box = jnp.where(inside, box_index([x, y, z], total_bits), 0)
                data = gathered[box >> 1, box & 1]
                data = jnp.where(inside, data, jnp.zeros_like(data))
                for lz in range(2):
                    for ly in range(2):
                        at = (2 * by + ly) * window + bx * 2 * n_equiv
                        part = (2 * lz + ly) * 2 * n_equiv
                        region[1 + 2 * bz + lz, :, at : at + 2 * n_equiv] = data[
                            :, part : part + 2 * n_equiv
                        ]
    locals_ = []
    sums = [jnp.zeros((64, 2 * n_equiv), F32) for _ in range(2)]
    for a in range(7):
        left = region[a : a + 2].reshape(64, 6 * window)
        for ty in range(2):
            right = wide[a, (1 - ty) * window : (7 - ty) * window, :]
            sums[ty] = sums[ty] + jnp.dot(left, right, preferred_element_type=F32)
    n_points = out.shape[2]
    lane = lax.broadcasted_iota(jnp.int32, (32, 2 * n_equiv), 1)
    slot = lax.broadcasted_iota(jnp.int32, (32, n_points), 1)
    for tz in range(2):
        for ty in range(2):
            first = 4 * tz + 2 * ty
            local = (
                inherited[:, first * n_equiv : (first + 2) * n_equiv]
                + sums[ty][32 * tz : 32 * tz + 32]
            )
            left = jnp.concatenate(
                [jnp.where(lane < n_equiv, local, 0.0), jnp.where(lane < n_equiv, 0.0, local)], 0
            ).astype(BF16)
            right = shape[first : first + 2].reshape(2 * n_equiv, n_points)
            far = jnp.dot(left, right, preferred_element_type=F32)
            for tx in range(2):
                value = near[first + tx] + far[32 * tx : 32 * tx + 32]
                out[first + tx] = jnp.where(slot < counts[first + tx], value, 0.0)


def call(kernel, ins, outs, scratch=(), flops=0, seen=0, limit=56, **kwargs):
    return pl.pallas_call(
        kernel,
        out_shape=outs,
        in_specs=ins,
        out_specs=jax.tree.map(lambda _: VMEM, outs),
        scratch_shapes=list(scratch),
        compiler_params=pltpu.CompilerParams(vmem_limit_bytes=limit * MIB),
        cost_estimate=pl.CostEstimate(flops=flops, bytes_accessed=seen, transcendentals=0),
        **kwargs,
    )


def near_call(phase, low, high, targets, before):
    n_leaves = 2 * low.shape[0]
    ins = [VMEM] * (3 if before is None else 4)
    args = (low, high, targets) + (() if before is None else (before,))
    n_points = targets.shape[1]
    us = {"own": 14, "z": 7, "x": 10, "y": 15}[phase]
    return call(
        functools.partial(near_kernel, phase),
        ins,
        jax.ShapeDtypeStruct((8, 32, n_points), F32),
        [
            pltpu.VMEM((4 * n_leaves, FEATURES, CHUNK), BF16),
            pltpu.VMEM((n_leaves, CHUNK), jnp.int32),
            pltpu.SMEM((n_leaves, CHUNK), jnp.int32),
            pltpu.SMEM((64,), jnp.int32),
            pltpu.SemaphoreType.DMA,
        ],
        flops=us * 10**9,
        seen=us * 10**6,
        name="near_" + phase,
    )(*args)


def per_device(positions, charges, counts, check_to_equiv, up_child, down_child, translate):
    n_points = positions.shape[2]
    n_probe = charges.shape[1]
    n_devices = lax.axis_size(AXES)
    total_bits = n_devices.bit_length() - 1
    shape_of = jax.ShapeDtypeStruct
    half = shape_of((4, ROWS, CHUNK), BF16)
    low, high = call(
        pack_kernel, [SMEM, VMEM, VMEM], (half, half), seen=10**6, flops=10**9, name="pack"
    )(counts, positions, charges)
    move = functools.partial(shifted, total=total_bits)
    z_low = move(high, 2, 1)
    z_high = move(low, 2, -1)
    targets, shape, equiv = call(
        upward_kernel,
        [VMEM] * 4,
        (
            shape_of((8, n_points, FEATURES), BF16),
            shape_of((8, 64, n_points), BF16),
            shape_of((n_probe, 512), BF16),
        ),
        seen=3 * 10**6,
        flops=3 * 10**9,
        name="upward",
    )(low, high, positions, check_to_equiv)
    gathered = lax.all_gather(equiv, AXES, axis=0)
    near = near_call("own", low, high, targets, None)
    planes = [a.reshape(2, 2, ROWS, CHUNK) for a in (z_low, low, high, z_high)]
    face = lambda x: jnp.stack([a[:, x] for a in planes]).reshape(8, ROWS, CHUNK)
    x_low = move(face(1), 0, 1)
    x_high = move(face(0), 0, -1)
    near = near_call("z", z_low, z_high, targets, near)

    def y_face(y):
        rows = []
        for z in range(4):
            rows += [x_low[2 * z + y][None], planes[z][y], x_high[2 * z + y][None]]
        return jnp.concatenate(rows, 0)

    y_low = move(y_face(1), 1, 1)
    y_high = move(y_face(0), 1, -1)
    near = near_call("x", x_low, x_high, targets, near)
    wide, down = call(
        widen_kernel,
        [VMEM, VMEM],
        (shape_of((7, 7 * 384, 128), BF16), shape_of((64, 512), BF16)),
        seen=5 * 10**6,
        flops=5 * 10**9,
        name="widen",
    )(translate, down_child)
    near = near_call("y", y_low, y_high, targets, near)
    return call(
        functools.partial(far_kernel, total_bits),
        [SMEM] + [VMEM] * 6,
        shape_of((8, n_probe, n_points), F32),
        [
            pltpu.VMEM((n_devices // 2, n_probe, 128), BF16),
            pltpu.VMEM((8, n_probe, 36 * 64), BF16),
        ],
        seen=10 * 10**6,
        flops=8 * 10**9,
        name="far",
    )(
        counts,
        gathered.reshape(n_devices // 2, 2, n_probe, 512),
        wide,
        up_child,
        down,
        shape,
        near,
    )


def solution(mesh):
    split = P(AXES, None, None)
    return jax.shard_map(
        per_device,
        mesh=mesh,
        in_specs=(split, split, P(AXES), P(), P(), P(), P()),
        out_specs=split,
        check_vma=False,
    )
```

```python
import functools

import jax
import jax.numpy as jnp
from jax import lax
from jax.experimental import pallas as pl
from jax.experimental.pallas import tpu as pltpu
from jax.sharding import PartitionSpec as P

AXES = ("oct", "leaf")
KERNEL_SCALE = 0.02
SOFTENING = 0.01
INVERSE = 1.0 / KERNEL_SCALE**2
CHUNK = 128
ROWS = 144
FEATURES = 48
MIB = 1 << 20
F32 = jnp.float32
BF16 = jnp.bfloat16
VMEM = pl.BlockSpec(memory_space=pltpu.VMEM)
SMEM = pl.BlockSpec(memory_space=pltpu.SMEM)


def bit_counts(total):
    return [(total + 2) // 3, (total + 1) // 3, total // 3]


def box_coords(index, total):
    coords = []
    for j, bits in enumerate(bit_counts(total)):
        value = 0
        for k in range(bits):
            value = value + ((index >> (3 * k + j)) & 1) * 2**k
        coords.append(value)
    return coords


def box_index(coords, total):
    index = 0
    for j, bits in enumerate(bit_counts(total)):
        for k in range(bits):
            index = index + ((coords[j] >> k) & 1) * 2 ** (3 * k + j)
    return index


def shifted(value, axis, step, total):
    pairs = []
    for device in range(2**total):
        coords = box_coords(device, total)
        coords[axis] += step
        if 0 <= coords[axis] < 2 ** bit_counts(total)[axis]:
            pairs.append((device, box_index(coords, total)))
    return lax.ppermute(value, AXES, pairs)


def pieces(x):
    first = x.astype(BF16).astype(F32)
    rest = x - first
    second = rest.astype(BF16).astype(F32)
    third = (rest - second).astype(BF16).astype(F32)
    return first, second, third


def row_index(shape):
    return lax.broadcasted_iota(jnp.int32, shape, 0)


def placed(rows, offsets):
    eight = jnp.concatenate([rows, jnp.zeros_like(rows)], 0)
    index = row_index(eight.shape)
    shift = jnp.where(index == 0, offsets[0], jnp.where(index == 1, offsets[1], offsets[2]))
    return jnp.where(index < 3, eight + shift, 0.0)


def with_rows(base, extra):
    index = row_index(base.shape)
    for k, row in enumerate(extra):
        base = jnp.where(index == 3 + k, row, base)
    return base


def source_features(rows, offsets):
    x = placed(rows, offsets)
    high = x.astype(BF16).astype(F32)
    low = x - high
    norm = INVERSE * jnp.sum(x * x, axis=0, keepdims=True)
    ones = (1.0, 1.0, 1.0)
    groups = [with_rows(high, pieces(norm)), with_rows(high, ones), high, low, low, low]
    return jnp.concatenate(groups, 0)


def target_features(rows, offsets):
    x = placed(rows, offsets)
    w1, w2, w3 = pieces((-2.0 * INVERSE) * x)
    norm = INVERSE * (jnp.sum(x * x, axis=0, keepdims=True) + SOFTENING)
    ones = (1.0, 1.0, 1.0)
    return jnp.concatenate(
        [with_rows(w1, ones), with_rows(w2, pieces(norm)), w3, w1, w2, w3], 0
    )


def pack_kernel(counts, positions, charges, low, high):
    n_points = positions.shape[2]
    n_chunks = n_points // CHUNK
    points = [positions[d].astype(F32) for d in range(3)]
    for leaf in range(8):
        out, at = (low, leaf) if leaf < 4 else (high, leaf - 4)
        count = counts[leaf]
        q = charges[leaf].astype(F32)
        slot = lax.broadcasted_iota(jnp.int32, q.shape, 1)
        q = jnp.where(slot < count, q, 0.0).astype(BF16)
        live = lax.shift_right_logical(count + (CHUNK - 1), 7).astype(F32)
        p = jnp.concatenate([points[d][leaf : leaf + 1] for d in range(3)], 0)
        rows = []
        for j in range(n_chunks):
            out[at, 32 * j : 32 * j + 32, :] = q[:, CHUNK * j : CHUNK * (j + 1)]
            rows.append(p[:, CHUNK * j : CHUNK * (j + 1)])
            rows.append(jnp.full((1, CHUNK), live, F32))
        out[at, 128:144, :] = jnp.concatenate(rows, 0).astype(BF16)


def upward_kernel(low, high, positions, to_equiv, targets, shape_out, equiv_out):
    n_points = positions.shape[2]
    n_chunks = n_points // CHUNK
    index = lax.broadcasted_iota(jnp.int32, (64, n_points), 0)
    surface = [
        ((index >> (2 * d)) & 3).astype(F32) * 0.5 - 0.25 for d in range(3)
    ]
    upward = []
    points = [positions[d].astype(F32) for d in range(3)]
    for leaf in range(8):
        src, at = (low, leaf) if leaf < 4 else (high, leaf - 4)
        p = [points[d][leaf : leaf + 1] for d in range(3)]
        square = (surface[0] - p[0]) ** 2
        square = square + (surface[1] - p[1]) ** 2
        square = square + (surface[2] - p[2]) ** 2
        shape = (KERNEL_SCALE * lax.rsqrt(square + SOFTENING)).astype(BF16)
        shape_out[leaf] = shape
        q = jnp.concatenate([src[at, 32 * j : 32 * j + 32, :] for j in range(n_chunks)], 1)
        upward.append(
            lax.dot_general(q, shape, (((1,), (1,)), ((), ())), preferred_element_type=F32)
        )
        offsets = (leaf % 2 - 1.0, leaf // 2 % 2 - 1.0, leaf // 4 - 1.0)
        block = src[at, 128:144, :].astype(F32)
        for j in range(n_chunks):
            features = target_features(block[4 * j : 4 * j + 4], offsets)
            targets[leaf, CHUNK * j : CHUNK * (j + 1), :] = features.T.astype(BF16)
    total = jnp.concatenate(upward, 0)
    equiv = jnp.zeros(total.shape, F32)
    for piece in pieces(total)[::-1]:
        equiv = equiv + jnp.dot(piece.astype(BF16), to_equiv[...], preferred_element_type=F32)
    equiv = equiv.astype(BF16)
    equiv_out[...] = jnp.concatenate([equiv[32 * l : 32 * l + 32] for l in range(8)], 1)


def near_kernel(phase, *refs):
    if phase == "own":
        low, high, targets, out, features, live_v, live_s, queue, sem = refs
    else:
        low, high, targets, before, out, features, live_v, live_s, queue, sem = refs
    per_side = low.shape[0]
    n_targets = targets.shape[1]

    def prepare(side):
        source = (low, high)[side]

        def one(leaf, _):
            block = source[leaf, 128:144, :].astype(F32)
            if phase == "own":
                z, y, x = side + 1, (leaf >> 1) + 1, (leaf & 1) + 1
            elif phase == "z":
                z, y, x = 3 * side, (leaf >> 1) + 1, (leaf & 1) + 1
            elif phase == "x":
                z, y, x = leaf >> 1, (leaf & 1) + 1, 3 * side
            else:
                z, y, x = leaf >> 2, 3 * side, leaf & 3
            offsets = [jnp.asarray(c - 2, jnp.int32).astype(F32) for c in (x, y, z)]
            at = side * per_side + leaf
            for j in range(4):
                features[4 * at + j] = source_features(block[4 * j : 4 * j + 4], offsets).astype(
                    BF16
                )
            live_v[pl.ds(at, 1), :] = block[3:4].astype(jnp.int32)
            return 0

        lax.fori_loop(0, per_side, one, 0)

    prepare(0)
    prepare(1)
    copy = pltpu.make_async_copy(live_v, live_s, sem)
    copy.start()
    copy.wait()
    if phase == "own":
        out[...] = jnp.zeros_like(out)
    else:
        out[...] = before[...]

    def run(side, leaves, target_leaves, width):
        total = jnp.int32(0)
        for leaf in leaves:
            n_live = live_s[leaf, 0]
            for j in range(4):
                queue[total] = 4 * leaf + j
                total = total + (j < n_live).astype(jnp.int32)
        rows = jnp.concatenate([targets[t] for t in target_leaves], 0)

        def block(c, _):
            us, qs = [], []
            for k in range(width):
                at = c * width + k
                item = jnp.where(at < total, queue[jnp.minimum(at, 63)], 4 * leaves[0])
                us.append(features[item])
                leaf, part = item >> 2, pl.multiple_of((item & 3) * 32, 32)
                if side is None:
                    q = jnp.where(
                        leaf < per_side,
                        low[jnp.minimum(leaf, per_side - 1), pl.ds(part, 32), :],
                        high[jnp.maximum(leaf - per_side, 0), pl.ds(part, 32), :],
                    )
                else:
                    q = (low, high)[side][leaf - side * per_side, pl.ds(part, 32), :]
                qs.append(jnp.where(at < total, q, jnp.zeros_like(q)))
            u = jnp.concatenate(us, 1)
            q = jnp.concatenate(qs, 1)
            square = jnp.dot(rows, u, preferred_element_type=F32)
            kern = lax.rsqrt(square).astype(BF16)
            added = lax.dot_general(q, kern, (((1,), (1,)), ((), ())), preferred_element_type=F32)
            for i, t in enumerate(target_leaves):
                out[t] += added[:, n_targets * i : n_targets * (i + 1)]
            return 0

        lax.fori_loop(0, (total + width - 1) // width, block, 0)

    if phase == "own":
        def half(h, _):
            run(None, list(range(8)), [4 * h + i for i in range(4)], 4)
            return 0

        lax.fori_loop(0, 2, half, 0)
    elif phase == "z":
        for side in range(2):
            run(side, [4 * side + i for i in range(4)], [4 * side + i for i in range(4)], 4)
    elif phase == "x":
        for side in range(2):

            def part(tz, _, side=side):
                leaves = [8 * side + 2 * tz + i for i in range(6)]
                run(side, leaves, [4 * tz + side, 4 * tz + 2 + side], 4)
                return 0

            lax.fori_loop(0, 2, part, 0)
    else:
        for side in range(2):

            def part(i, _, side=side):
                tz, tx = i >> 1, i & 1
                leaves = [
                    16 * side + 4 * (tz + dz) + tx + dx for dz in range(3) for dx in range(3)
                ]
                run(side, leaves, [4 * tz + 2 * side + tx], 8)
                return 0

            lax.fori_loop(0, 4, part, 0)


def far_kernel(
    total_bits,
    counts,
    gathered_hbm,
    table_hbm,
    up,
    down,
    shape,
    near,
    out,
    gathered,
    table,
    boxes,
    region,
    sems,
):
    n_equiv = 64
    span = 7 * n_equiv
    window = 6 * n_equiv
    bits = bit_counts(total_bits)
    n_pairs = gathered.shape[0]
    step = n_pairs // 4
    copies = []
    for i in range(4):
        part = pl.ds(step * i, step)
        copies.append(pltpu.make_async_copy(gathered_hbm.at[part], gathered.at[part], sems.at[i]))
    copies.append(pltpu.make_async_copy(table_hbm, table, sems.at[4]))
    for copy in copies:
        copy.start()
    me = lax.axis_index("oct") * lax.axis_size("leaf") + lax.axis_index("leaf")
    cx, cy, cz = box_coords(me, total_bits)
    zeros_up = jnp.zeros((8 * n_equiv, n_equiv), F32)
    up_rows = up[...].astype(F32).reshape(8 * n_equiv, n_equiv)
    up_even = jnp.concatenate([up_rows, zeros_up], 1).astype(BF16)
    up_odd = jnp.concatenate([zeros_up, up_rows], 1).astype(BF16)
    for i in range(4):
        copies[i].wait()
        at = slice(step * i, step * (i + 1))
        even = gathered[at, 0].reshape(step * 32, 8 * n_equiv)
        odd = gathered[at, 1].reshape(step * 32, 8 * n_equiv)
        both = jnp.dot(even, up_even, preferred_element_type=F32)
        both = both + jnp.dot(odd, up_odd, preferred_element_type=F32)
        boxes[at] = both.astype(BF16).reshape(step, 32, 2 * n_equiv)

    region[:, 0] = jnp.zeros_like(region[:, 0])
    region[:, 7] = jnp.zeros_like(region[:, 7])
    nothing = jnp.zeros((32, n_equiv), BF16)
    for bz in range(3):
        for by in range(3):
            data = []
            for bx in range(3):
                z, y, x = cz + bz - 1, cy + by - 1, cx + bx - 1
                inside = (
                    (z >= 0)
                    & (z < 2 ** bits[2])
                    & (y >= 0)
                    & (y < 2 ** bits[1])
                    & (x >= 0)
                    & (x < 2 ** bits[0])
                )
                box = jnp.where(inside, box_index([x, y, z], total_bits), 0)
                value = gathered[box >> 1, box & 1]
                data.append(jnp.where(inside, value, jnp.zeros_like(value)))
            for lz in range(2):
                rows = []
                for ly in range(2):
                    part = (2 * lz + ly) * 2 * n_equiv
                    rows.append(
                        jnp.concatenate([d[:, part : part + 2 * n_equiv] for d in data], 1)
                    )
                at = slice(2 * by * span, (2 * by + 2) * span)
                plane = 1 + 2 * bz + lz
                region[0, plane, :, at] = jnp.concatenate([nothing, rows[0], nothing, rows[1]], 1)
                region[1, plane, :, at] = jnp.concatenate([rows[0], nothing, rows[1], nothing], 1)
    copies[4].wait()
    for a in (2, 3, 4):
        for b in (2, 3, 4):
            at = b * span + 2 * n_equiv
            table[a, at : at + 3 * n_equiv, :] = jnp.zeros((3 * n_equiv, n_equiv), BF16)

    parent = cx >> 1
    skip = n_equiv * (1 - (cx & 1))
    total = jnp.zeros((32, n_equiv), F32)
    zero = jnp.zeros((32, 2 * n_equiv), BF16)
    for z in range(2 ** bits[2]):
        left, right = [], []
        for y in range(2 ** bits[1]):
            for dx in (-1, 0, 1):
                px = parent + dx
                inside = (px >= 0) & (px < 2 ** (bits[0] - 1))
                pair = box_index([2 * jnp.where(inside, px, 0), y, z], total_bits) >> 1
                left.append(jnp.where(inside, boxes[pair], zero))
            start = pl.multiple_of((y - cy + 3) * span + skip, n_equiv)
            right.append(table[z - cz + 3, pl.ds(start, window), :])
        total = total + jnp.dot(
            jnp.concatenate(left, 1), jnp.concatenate(right, 0), preferred_element_type=F32
        )
    box_local = (0.5 * total).astype(BF16)
    inherited = jnp.dot(box_local, down[...], preferred_element_type=F32)

    sums = [jnp.zeros((128, n_equiv), F32) for _ in range(2)]
    for a in range(7):
        left = jnp.concatenate(
            [region[tx, a : a + 2].reshape(64, 6 * span) for tx in range(2)], 0
        )
        for ty in range(2):
            right = table[a, (1 - ty) * span : (7 - ty) * span, :]
            sums[ty] = sums[ty] + jnp.dot(left, right, preferred_element_type=F32)
    n_points = out.shape[2]
    slot = lax.broadcasted_iota(jnp.int32, (32, n_points), 1)
    gap = jnp.zeros((32, n_equiv), F32)
    for tz in range(2):
        for ty in range(2):
            first = 4 * tz + 2 * ty
            local = [
                inherited[:, (first + tx) * n_equiv : (first + tx + 1) * n_equiv]
                + sums[ty][64 * tx + 32 * tz : 64 * tx + 32 * tz + 32]
                for tx in range(2)
            ]
            left = jnp.concatenate(
                [jnp.concatenate([local[0], gap], 1), jnp.concatenate([gap, local[1]], 1)], 0
            ).astype(BF16)
            right = shape[first : first + 2].reshape(2 * n_equiv, n_points)
            far = jnp.dot(left, right, preferred_element_type=F32)
            for tx in range(2):
                value = near[first + tx] + far[32 * tx : 32 * tx + 32]
                out[first + tx] = jnp.where(slot < counts[first + tx], value, 0.0)


def call(kernel, ins, outs, scratch=(), flops=0, seen=0, limit=56, **kwargs):
    return pl.pallas_call(
        kernel,
        out_shape=outs,
        in_specs=ins,
        out_specs=jax.tree.map(lambda _: VMEM, outs),
        scratch_shapes=list(scratch),
        compiler_params=pltpu.CompilerParams(vmem_limit_bytes=limit * MIB),
        cost_estimate=pl.CostEstimate(flops=flops, bytes_accessed=seen, transcendentals=0),
        **kwargs,
    )


def near_call(phase, low, high, targets, before):
    n_leaves = 2 * low.shape[0]
    ins = [VMEM] * (3 if before is None else 4)
    args = (low, high, targets) + (() if before is None else (before,))
    n_points = targets.shape[1]
    us = {"own": 14, "z": 7, "x": 10, "y": 15}[phase]
    return call(
        functools.partial(near_kernel, phase),
        ins,
        jax.ShapeDtypeStruct((8, 32, n_points), F32),
        [
            pltpu.VMEM((4 * n_leaves, FEATURES, CHUNK), BF16),
            pltpu.VMEM((n_leaves, CHUNK), jnp.int32),
            pltpu.SMEM((n_leaves, CHUNK), jnp.int32),
            pltpu.SMEM((64,), jnp.int32),
            pltpu.SemaphoreType.DMA,
        ],
        flops=us * 10**9,
        seen=us * 10**6,
        name="near_" + phase,
    )(*args)


def per_device(positions, charges, counts, check_to_equiv, up_child, down_child, translate):
    n_points = positions.shape[2]
    n_probe = charges.shape[1]
    n_devices = lax.axis_size(AXES)
    total_bits = n_devices.bit_length() - 1
    shape_of = jax.ShapeDtypeStruct
    half = shape_of((4, ROWS, CHUNK), BF16)
    positions = positions.transpose(1, 0, 2)
    low, high = call(
        pack_kernel, [SMEM, VMEM, VMEM], (half, half), seen=10**6, flops=10**9, name="pack"
    )(counts, positions, charges)
    move = functools.partial(shifted, total=total_bits)
    z_low = move(high, 2, 1)
    z_high = move(low, 2, -1)
    targets, shape, equiv = call(
        upward_kernel,
        [VMEM] * 4,
        (
            shape_of((8, n_points, FEATURES), BF16),
            shape_of((8, 64, n_points), BF16),
            shape_of((n_probe, 512), BF16),
        ),
        seen=3 * 10**6,
        flops=3 * 10**9,
        name="upward",
    )(low, high, positions, check_to_equiv)
    gathered = lax.all_gather(equiv, AXES, axis=0)
    planes = [a.reshape(2, 2, ROWS, CHUNK) for a in (z_low, low, high, z_high)]
    faces = [jnp.stack([a[:, x] for a in planes]).reshape(8, ROWS, CHUNK) for x in range(2)]
    faces[0], faces[1], targets = lax.optimization_barrier((faces[0], faces[1], targets))
    x_low = move(faces[1], 0, 1)
    x_high = move(faces[0], 0, -1)
    near = near_call("own", low, high, targets, None)
    x_low, x_high, near = lax.optimization_barrier((x_low, x_high, near))

    def y_face(y):
        rows = []
        for z in range(4):
            rows += [x_low[2 * z + y][None], planes[z][y], x_high[2 * z + y][None]]
        return jnp.concatenate(rows, 0)

    faces = [y_face(y) for y in range(2)]
    faces[0], faces[1], near = lax.optimization_barrier((faces[0], faces[1], near))
    y_low = move(faces[1], 1, 1)
    y_high = move(faces[0], 1, -1)
    near = near_call("z", z_low, z_high, targets, near)
    near = near_call("x", x_low, x_high, targets, near)
    translate, near = lax.optimization_barrier((translate, near))
    table = translate.reshape(7, 7 * 7 * 64, 64)
    table, near, y_low, y_high = lax.optimization_barrier((table, near, y_low, y_high))
    near = near_call("y", y_low, y_high, targets, near)
    down = down_child.transpose(1, 0, 2).reshape(64, 512)
    anywhere = pl.BlockSpec(memory_space=pl.ANY)
    return call(
        functools.partial(far_kernel, total_bits),
        [SMEM, anywhere, anywhere] + [VMEM] * 4,
        shape_of((8, n_probe, n_points), F32),
        [
            pltpu.VMEM((n_devices // 2, 2, n_probe, 512), BF16),
            pltpu.VMEM((7, 7 * 7 * 64, 64), BF16),
            pltpu.VMEM((n_devices // 2, n_probe, 128), BF16),
            pltpu.VMEM((2, 8, n_probe, 6 * 7 * 64), BF16),
            pltpu.SemaphoreType.DMA((5,)),
        ],
        seen=10 * 10**6,
        flops=8 * 10**9,
        name="far",
    )(
        counts,
        gathered.reshape(n_devices // 2, 2, n_probe, 512),
        table,
        up_child,
        down,
        shape,
        near,
    )


def solution(mesh):
    split = P(AXES, None, None)
    return jax.shard_map(
        per_device,
        mesh=mesh,
        in_specs=(split, split, P(AXES), P(), P(), P(), P()),
        out_specs=split,
        check_vma=False,
    )
```

```python
import functools

import jax
import jax.numpy as jnp
import numpy as np
from jax import lax
from jax.experimental import pallas as pl
from jax.experimental.pallas import tpu as pltpu
from jax.sharding import PartitionSpec as P

AXES = ("oct", "leaf")
KERNEL_SCALE = 0.02
SOFTENING = 0.01
INVERSE = 1.0 / KERNEL_SCALE**2
CHUNK = 128
ROWS = 144
FEATURES = 48
MIB = 1 << 20
F32 = jnp.float32
BF16 = jnp.bfloat16
VMEM = pl.BlockSpec(memory_space=pltpu.VMEM)
SMEM = pl.BlockSpec(memory_space=pltpu.SMEM)


def bit_counts(total):
    return [(total + 2) // 3, (total + 1) // 3, total // 3]


def box_coords(index, total):
    coords = []
    for j, bits in enumerate(bit_counts(total)):
        value = 0
        for k in range(bits):
            value = value + ((index >> (3 * k + j)) & 1) * 2**k
        coords.append(value)
    return coords


def box_index(coords, total):
    index = 0
    for j, bits in enumerate(bit_counts(total)):
        for k in range(bits):
            index = index + ((coords[j] >> k) & 1) * 2 ** (3 * k + j)
    return index


def shifted(value, axis, step, total):
    pairs = []
    for device in range(2**total):
        coords = box_coords(device, total)
        coords[axis] += step
        if 0 <= coords[axis] < 2 ** bit_counts(total)[axis]:
            pairs.append((device, box_index(coords, total)))
    return lax.ppermute(value, AXES, pairs)


def pieces(x):
    first = x.astype(BF16).astype(F32)
    rest = x - first
    second = rest.astype(BF16).astype(F32)
    third = (rest - second).astype(BF16).astype(F32)
    return first, second, third


def row_index(shape):
    return lax.broadcasted_iota(jnp.int32, shape, 0)


def placed(rows, offsets):
    eight = jnp.concatenate([rows, jnp.zeros_like(rows)], 0)
    index = row_index(eight.shape)
    shift = jnp.where(index == 0, offsets[0], jnp.where(index == 1, offsets[1], offsets[2]))
    return jnp.where(index < 3, eight + shift, 0.0)


def with_rows(base, extra):
    index = row_index(base.shape)
    for k, row in enumerate(extra):
        base = jnp.where(index == 3 + k, row, base)
    return base


def source_features(rows, offsets):
    x = placed(rows, offsets)
    high = x.astype(BF16).astype(F32)
    low = x - high
    norm = INVERSE * jnp.sum(x * x, axis=0, keepdims=True)
    ones = (1.0, 1.0, 1.0)
    groups = [with_rows(high, pieces(norm)), with_rows(high, ones), high, low, low, low]
    return jnp.concatenate(groups, 0)


def target_features(rows, offsets):
    x = placed(rows, offsets)
    w1, w2, w3 = pieces((-2.0 * INVERSE) * x)
    norm = INVERSE * (jnp.sum(x * x, axis=0, keepdims=True) + SOFTENING)
    ones = (1.0, 1.0, 1.0)
    return jnp.concatenate(
        [with_rows(w1, ones), with_rows(w2, pieces(norm)), w3, w1, w2, w3], 0
    )


def pack_kernel(counts, positions, charges, low, high):
    n_points = positions.shape[2]
    n_chunks = n_points // CHUNK
    points = [positions[d].astype(F32) for d in range(3)]
    for leaf in range(8):
        out, at = (low, leaf) if leaf < 4 else (high, leaf - 4)
        count = counts[leaf]
        q = charges[leaf].astype(F32)
        slot = lax.broadcasted_iota(jnp.int32, q.shape, 1)
        q = jnp.where(slot < count, q, 0.0).astype(BF16)
        live = lax.shift_right_logical(count + (CHUNK - 1), 7).astype(F32)
        p = jnp.concatenate([points[d][leaf : leaf + 1] for d in range(3)], 0)
        rows = []
        for j in range(n_chunks):
            out[at, 32 * j : 32 * j + 32, :] = q[:, CHUNK * j : CHUNK * (j + 1)]
            rows.append(p[:, CHUNK * j : CHUNK * (j + 1)])
            rows.append(jnp.full((1, CHUNK), live, F32))
        out[at, 128:144, :] = jnp.concatenate(rows, 0).astype(BF16)


def upward_kernel(low, high, positions, to_equiv, targets, shape_out, equiv_out):
    n_points = positions.shape[2]
    n_chunks = n_points // CHUNK
    index = lax.broadcasted_iota(jnp.int32, (64, n_points), 0)
    surface = [
        ((index >> (2 * d)) & 3).astype(F32) * 0.5 - 0.25 for d in range(3)
    ]
    upward = []
    points = [positions[d].astype(F32) for d in range(3)]
    for leaf in range(8):
        src, at = (low, leaf) if leaf < 4 else (high, leaf - 4)
        p = [points[d][leaf : leaf + 1] for d in range(3)]
        square = (surface[0] - p[0]) ** 2
        square = square + (surface[1] - p[1]) ** 2
        square = square + (surface[2] - p[2]) ** 2
        shape = (KERNEL_SCALE * lax.rsqrt(square + SOFTENING)).astype(BF16)
        shape_out[leaf] = shape
        q = jnp.concatenate([src[at, 32 * j : 32 * j + 32, :] for j in range(n_chunks)], 1)
        upward.append(
            lax.dot_general(q, shape, (((1,), (1,)), ((), ())), preferred_element_type=F32)
        )
        offsets = (leaf % 2 - 1.0, leaf // 2 % 2 - 1.0, leaf // 4 - 1.0)
        block = src[at, 128:144, :].astype(F32)
        for j in range(n_chunks):
            features = target_features(block[4 * j : 4 * j + 4], offsets)
            targets[4 * leaf + j] = features.T.astype(BF16)
    total = jnp.concatenate(upward, 0)
    equiv = jnp.zeros(total.shape, F32)
    for piece in pieces(total)[::-1]:
        equiv = equiv + jnp.dot(piece.astype(BF16), to_equiv[...], preferred_element_type=F32)
    equiv = equiv.astype(BF16)
    equiv_out[...] = jnp.concatenate([equiv[32 * l : 32 * l + 32] for l in range(8)], 1)


def near_kernel(sides, with_before, leaves, sources, aims, *refs):
    payloads, refs = refs[: len(sides)], refs[len(sides) :]
    targets, refs = refs[0], refs[1:]
    if with_before:
        before, refs = refs[0], refs[1:]
    counts, out, features, values, live_v, live_s, queue, aim_queue, sem = refs
    n_leaves = sum(sides)
    n_tasks, n_sources = sources.shape
    n_aims = aims.shape[1]
    first = 0
    for payload, size in zip(payloads, sides):

        def one(leaf, _, payload=payload, first=first):
            block = payload[leaf, 128:144, :].astype(F32)
            at = first + leaf
            offsets = [leaves[at, d].astype(F32) for d in range(3)]
            for j in range(4):
                features[4 * at + j] = source_features(block[4 * j : 4 * j + 4], offsets).astype(
                    BF16
                )
                values[4 * at + j] = payload[leaf, 32 * j : 32 * j + 32, :]
            live_v[pl.ds(at, 1), :] = block[3:4].astype(jnp.int32)
            return 0

        lax.fori_loop(0, size, one, 0)
        first += size
    features[4 * n_leaves] = features[0]
    values[4 * n_leaves] = jnp.zeros((32, CHUNK), BF16)
    copy = pltpu.make_async_copy(live_v, live_s, sem)
    copy.start()
    copy.wait()
    out[...] = before[...] if with_before else jnp.zeros_like(out)

    def compute(start, n_rows, n_items):
        places = [aim_queue[start + i] for i in range(n_rows)]
        rows = jnp.concatenate([targets[place] for place in places], 0)

        def add(at, width, total):
            items = [queue[at + k] for k in range(width)]
            u = jnp.concatenate([features[item] for item in items], 1)
            q = jnp.concatenate([values[item] for item in items], 1)
            square = jnp.dot(rows, u, preferred_element_type=F32)
            kern = lax.rsqrt(square).astype(BF16)
            return total + lax.dot_general(
                q, kern, (((1,), (1,)), ((), ())), preferred_element_type=F32
            )

        def store(total):
            for i, place in enumerate(places):
                out[place] += total[:, CHUNK * i : CHUNK * (i + 1)]

        full = n_items // 12
        rest = n_items - 12 * full
        total = lax.fori_loop(
            0, full, lambda c, t: add(12 * c, 12, t), jnp.zeros((32, CHUNK * n_rows), F32)
        )
        store(total)
        for width in (4, 8, 12):

            @pl.when((rest > width - 4) & (rest <= width))
            def _(width=width):
                store(add(12 * full, width, jnp.zeros((32, CHUNK * n_rows), F32)))

    def task(i, _):
        n_items = jnp.int32(0)
        for k in range(n_sources):
            leaf = sources[i, k]
            n_live = jnp.where(leaf >= 0, live_s[jnp.maximum(leaf, 0), 0], 0)
            for j in range(4):
                queue[n_items] = 4 * leaf + j
                n_items = n_items + (j < n_live).astype(jnp.int32)
        for k in range(12):
            queue[n_items + k] = 4 * n_leaves
        n_rows = jnp.int32(0)
        for k in range(n_aims):
            leaf = aims[i, k]
            count = jnp.where(leaf >= 0, counts[jnp.maximum(leaf, 0)], 0)
            for j in range(4):
                aim_queue[n_rows] = 4 * leaf + j
                n_rows = n_rows + (CHUNK * j < count).astype(jnp.int32)

        @pl.when(n_items > 0)
        def _():
            full = n_rows // 4

            def four(c, _):
                compute(4 * c, 4, n_items)
                return 0

            lax.fori_loop(0, full, four, 0)
            for rest in (1, 2, 3):

                @pl.when(n_rows - 4 * full == rest)
                def _(rest=rest):
                    compute(4 * full, rest, n_items)

        return 0

    lax.fori_loop(0, n_tasks, task, 0)


def faces_kernel(x_low, z_low, low, high, z_high, x_high, *faces):
    for y in range(2):
        for z, plane in enumerate((z_low, low, high, z_high)):
            faces[y][4 * z] = x_low[2 * z + y]
            faces[y][4 * z + 1] = plane[2 * y]
            faces[y][4 * z + 2] = plane[2 * y + 1]
            faces[y][4 * z + 3] = x_high[2 * z + y]


def far_kernel(
    total_bits,
    counts,
    gathered_hbm,
    table_hbm,
    up,
    down,
    shape,
    near,
    out,
    gathered,
    table,
    boxes,
    region,
    sems,
):
    n_equiv = 64
    span = 7 * n_equiv
    window = 6 * n_equiv
    bits = bit_counts(total_bits)
    n_pairs = gathered.shape[0]
    step = n_pairs // 4
    copies = []
    for i in range(4):
        part = pl.ds(step * i, step)
        copies.append(pltpu.make_async_copy(gathered_hbm.at[part], gathered.at[part], sems.at[i]))
    copies.append(pltpu.make_async_copy(table_hbm, table, sems.at[4]))
    for copy in copies:
        copy.start()
    me = lax.axis_index("oct") * lax.axis_size("leaf") + lax.axis_index("leaf")
    cx, cy, cz = box_coords(me, total_bits)
    zeros_up = jnp.zeros((8 * n_equiv, n_equiv), F32)
    up_rows = up[...].astype(F32).reshape(8 * n_equiv, n_equiv)
    up_even = jnp.concatenate([up_rows, zeros_up], 1).astype(BF16)
    up_odd = jnp.concatenate([zeros_up, up_rows], 1).astype(BF16)
    for i in range(4):
        copies[i].wait()
        at = slice(step * i, step * (i + 1))
        even = gathered[at, 0].reshape(step * 32, 8 * n_equiv)
        odd = gathered[at, 1].reshape(step * 32, 8 * n_equiv)
        both = jnp.dot(even, up_even, preferred_element_type=F32)
        both = both + jnp.dot(odd, up_odd, preferred_element_type=F32)
        boxes[at] = both.astype(BF16).reshape(step, 32, 2 * n_equiv)

    region[:, 0] = jnp.zeros_like(region[:, 0])
    region[:, 7] = jnp.zeros_like(region[:, 7])
    nothing = jnp.zeros((32, n_equiv), BF16)
    for bz in range(3):
        for by in range(3):
            data = []
            for bx in range(3):
                z, y, x = cz + bz - 1, cy + by - 1, cx + bx - 1
                inside = (
                    (z >= 0)
                    & (z < 2 ** bits[2])
                    & (y >= 0)
                    & (y < 2 ** bits[1])
                    & (x >= 0)
                    & (x < 2 ** bits[0])
                )
                box = jnp.where(inside, box_index([x, y, z], total_bits), 0)
                value = gathered[box >> 1, box & 1]
                data.append(jnp.where(inside, value, jnp.zeros_like(value)))
            for lz in range(2):
                rows = []
                for ly in range(2):
                    part = (2 * lz + ly) * 2 * n_equiv
                    rows.append(
                        jnp.concatenate([d[:, part : part + 2 * n_equiv] for d in data], 1)
                    )
                at = slice(2 * by * span, (2 * by + 2) * span)
                plane = 1 + 2 * bz + lz
                region[0, plane, :, at] = jnp.concatenate([nothing, rows[0], nothing, rows[1]], 1)
                region[1, plane, :, at] = jnp.concatenate([rows[0], nothing, rows[1], nothing], 1)
    copies[4].wait()
    for a in (2, 3, 4):
        for b in (2, 3, 4):
            at = b * span + 2 * n_equiv
            table[a, at : at + 3 * n_equiv, :] = jnp.zeros((3 * n_equiv, n_equiv), BF16)

    parent = cx >> 1
    skip = n_equiv * (1 - (cx & 1))
    total = jnp.zeros((32, n_equiv), F32)
    zero = jnp.zeros((32, 2 * n_equiv), BF16)
    for z in range(2 ** bits[2]):
        left, right = [], []
        for y in range(2 ** bits[1]):
            for dx in (-1, 0, 1):
                px = parent + dx
                inside = (px >= 0) & (px < 2 ** (bits[0] - 1))
                pair = box_index([2 * jnp.where(inside, px, 0), y, z], total_bits) >> 1
                left.append(jnp.where(inside, boxes[pair], zero))
            start = pl.multiple_of((y - cy + 3) * span + skip, n_equiv)
            right.append(table[z - cz + 3, pl.ds(start, window), :])
        total = total + jnp.dot(
            jnp.concatenate(left, 1), jnp.concatenate(right, 0), preferred_element_type=F32
        )
    box_local = (0.5 * total).astype(BF16)
    down_row = jnp.concatenate([down[l] for l in range(8)], 1)
    inherited = jnp.dot(box_local, down_row, preferred_element_type=F32)

    sums = [jnp.zeros((128, n_equiv), F32) for _ in range(2)]
    for a in range(7):
        left = jnp.concatenate(
            [region[tx, a : a + 2].reshape(64, 6 * span) for tx in range(2)], 0
        )
        for ty in range(2):
            right = table[a, (1 - ty) * span : (7 - ty) * span, :]
            sums[ty] = sums[ty] + jnp.dot(left, right, preferred_element_type=F32)
    n_points = out.shape[2]
    slot = lax.broadcasted_iota(jnp.int32, (32, n_points), 1)
    gap = jnp.zeros((32, n_equiv), F32)
    for tz in range(2):
        for ty in range(2):
            first = 4 * tz + 2 * ty
            local = [
                inherited[:, (first + tx) * n_equiv : (first + tx + 1) * n_equiv]
                + sums[ty][64 * tx + 32 * tz : 64 * tx + 32 * tz + 32]
                for tx in range(2)
            ]
            left = jnp.concatenate(
                [jnp.concatenate([local[0], gap], 1), jnp.concatenate([gap, local[1]], 1)], 0
            ).astype(BF16)
            right = shape[first : first + 2].reshape(2 * n_equiv, n_points)
            far = jnp.dot(left, right, preferred_element_type=F32)
            for tx in range(2):
                value = jnp.concatenate([near[4 * (first + tx) + j] for j in range(4)], 1)
                value = value + far[32 * tx : 32 * tx + 32]
                out[first + tx] = jnp.where(slot < counts[first + tx], value, 0.0)


def call(kernel, ins, outs, scratch=(), flops=0, seen=0, limit=56, **kwargs):
    return pl.pallas_call(
        kernel,
        out_shape=outs,
        in_specs=ins,
        out_specs=jax.tree.map(lambda _: VMEM, outs),
        scratch_shapes=list(scratch),
        compiler_params=pltpu.CompilerParams(vmem_limit_bytes=limit * MIB),
        cost_estimate=pl.CostEstimate(flops=flops, bytes_accessed=seen, transcendentals=0),
        **kwargs,
    )


def near_tables():
    both = range(2)
    own = [(x, y, z) for z in (1, 2) for y in (1, 2) for x in (1, 2)]
    z_side = [(x, y, 3 * side) for side in both for y in (1, 2) for x in (1, 2)]
    x_side = [(3 * side, y, z) for side in both for z in range(4) for y in (1, 2)]
    y_side = [(x, 3 * side, z) for side in both for z in range(4) for x in range(4)]
    eight = list(range(8))
    middle = [(eight, [4, 5, 6, 7])]
    for side in both:
        four = [4 * side + i for i in range(4)]
        middle.append(([8 + leaf for leaf in four], four))
    for tx in both:
        for tz in both:
            six = [16 + 8 * tx + 2 * tz + i for i in range(6)]
            middle.append((six, [4 * tz + 2 * ty + tx for ty in both]))
    last = []
    for ty in both:
        for tz in both:
            for tx in both:
                nine = [
                    16 * ty + 4 * (tz + dz) + tx + dx for dz in range(3) for dx in range(3)
                ]
                last.append((nine, [4 * tz + 2 * ty + tx]))
    return {
        "first": ((4, 4), own, [(eight, [0, 1, 2, 3])]),
        "middle": ((4, 4, 4, 4, 8, 8), own + z_side + x_side, middle),
        "last": ((16, 16), y_side, last),
    }


def near_call(phase, payloads, targets, counts, before):
    sides, places, tasks = near_tables()[phase]
    n_leaves = sum(sides)
    n_sources = max(len(task[0]) for task in tasks)
    n_aims = max(len(task[1]) for task in tasks)
    pad = lambda row, size: row + [-1] * (size - len(row))
    tables = [
        np.array(places, np.int32) - 2,
        np.array([pad(task[0], n_sources) for task in tasks], np.int32),
        np.array([pad(task[1], n_aims) for task in tasks], np.int32),
    ]
    args = [jnp.asarray(table) for table in tables] + list(payloads) + [targets]
    if before is not None:
        args.append(before)
    args.append(counts)
    us = {"first": 12, "middle": 30, "last": 15}[phase]
    return call(
        functools.partial(near_kernel, sides, before is not None),
        [SMEM] * 3 + [VMEM] * (len(args) - 4) + [SMEM],
        jax.ShapeDtypeStruct((32, 32, CHUNK), F32),
        [
            pltpu.VMEM((4 * n_leaves + 1, FEATURES, CHUNK), BF16),
            pltpu.VMEM((4 * n_leaves + 1, 32, CHUNK), BF16),
            pltpu.VMEM((n_leaves, CHUNK), jnp.int32),
            pltpu.SMEM((n_leaves, CHUNK), jnp.int32),
            pltpu.SMEM((64,), jnp.int32),
            pltpu.SMEM((40,), jnp.int32),
            pltpu.SemaphoreType.DMA,
        ],
        flops=us * 10**9,
        seen=us * 10**6,
        name="near_" + phase,
    )(*args)


def per_device(positions, charges, counts, check_to_equiv, up_child, down_child, translate):
    n_points = positions.shape[2]
    n_probe = charges.shape[1]
    n_devices = lax.axis_size(AXES)
    total_bits = n_devices.bit_length() - 1
    shape_of = jax.ShapeDtypeStruct
    half = shape_of((4, ROWS, CHUNK), BF16)
    positions = positions.transpose(1, 0, 2)
    low, high = call(
        pack_kernel, [SMEM, VMEM, VMEM], (half, half), seen=10**6, flops=10**9, name="pack"
    )(counts, positions, charges)
    move = functools.partial(shifted, total=total_bits)
    z_low = move(high, 2, 1)
    z_high = move(low, 2, -1)
    targets, shape, equiv = call(
        upward_kernel,
        [VMEM] * 4,
        (
            shape_of((32, CHUNK, FEATURES), BF16),
            shape_of((8, 64, n_points), BF16),
            shape_of((n_probe, 512), BF16),
        ),
        seen=3 * 10**6,
        flops=3 * 10**9,
        name="upward",
    )(low, high, positions, check_to_equiv)
    gathered = lax.all_gather(equiv, AXES, axis=0)
    planes = [a.reshape(2, 2, ROWS, CHUNK) for a in (z_low, low, high, z_high)]
    faces = [jnp.stack([a[:, x] for a in planes]).reshape(8, ROWS, CHUNK) for x in range(2)]
    faces[0], faces[1], targets = lax.optimization_barrier((faces[0], faces[1], targets))
    x_low = move(faces[1], 0, 1)
    x_high = move(faces[0], 0, -1)
    near = near_call("first", (low, high), targets, counts, None)
    x_low, x_high, near = lax.optimization_barrier((x_low, x_high, near))
    plane = shape_of((16, ROWS, CHUNK), BF16)
    y_faces = call(
        faces_kernel, [VMEM] * 6, (plane, plane), seen=3 * 10**6, flops=10**9, name="faces"
    )(x_low, z_low, low, high, z_high, x_high)
    face_0, face_1, near = lax.optimization_barrier((*y_faces, near))
    y_low = move(face_1, 1, 1)
    y_high = move(face_0, 1, -1)
    near = near_call(
        "middle", (low, high, z_low, z_high, x_low, x_high), targets, counts, near
    )
    translate, near = lax.optimization_barrier((translate, near))
    table = translate.reshape(7, 7 * 7 * 64, 64)
    table, near, y_low, y_high = lax.optimization_barrier((table, near, y_low, y_high))
    near = near_call("last", (y_low, y_high), targets, counts, near)
    anywhere = pl.BlockSpec(memory_space=pl.ANY)
    return call(
        functools.partial(far_kernel, total_bits),
        [SMEM, anywhere, anywhere] + [VMEM] * 4,
        shape_of((8, n_probe, n_points), F32),
        [
            pltpu.VMEM((n_devices // 2, 2, n_probe, 512), BF16),
            pltpu.VMEM((7, 7 * 7 * 64, 64), BF16),
            pltpu.VMEM((n_devices // 2, n_probe, 128), BF16),
            pltpu.VMEM((2, 8, n_probe, 6 * 7 * 64), BF16),
            pltpu.SemaphoreType.DMA((5,)),
        ],
        seen=10 * 10**6,
        flops=8 * 10**9,
        name="far",
    )(
        counts,
        gathered.reshape(n_devices // 2, 2, n_probe, 512),
        table,
        up_child,
        down_child,
        shape,
        near,
    )


def solution(mesh):
    split = P(AXES, None, None)
    return jax.shard_map(
        per_device,
        mesh=mesh,
        in_specs=(split, split, P(AXES), P(), P(), P(), P()),
        out_specs=split,
        check_vma=False,
    )
```

```python
import functools

import jax
import jax.numpy as jnp
import numpy as np
from jax import lax
from jax.experimental import pallas as pl
from jax.experimental.pallas import tpu as pltpu
from jax.sharding import PartitionSpec as P

AXES = ("oct", "leaf")
KERNEL_SCALE = 0.02
SOFTENING = 0.01
INVERSE = 1.0 / KERNEL_SCALE**2
CHUNK = 128
ROWS = 144
FEATURES = 48
MIB = 1 << 20
F32 = jnp.float32
BF16 = jnp.bfloat16
VMEM = pl.BlockSpec(memory_space=pltpu.VMEM)
SMEM = pl.BlockSpec(memory_space=pltpu.SMEM)


def bit_counts(total):
    return [(total + 2) // 3, (total + 1) // 3, total // 3]


def box_coords(index, total):
    coords = []
    for j, bits in enumerate(bit_counts(total)):
        value = 0
        for k in range(bits):
            value = value + ((index >> (3 * k + j)) & 1) * 2**k
        coords.append(value)
    return coords


def box_index(coords, total):
    index = 0
    for j, bits in enumerate(bit_counts(total)):
        for k in range(bits):
            index = index + ((coords[j] >> k) & 1) * 2 ** (3 * k + j)
    return index


def shifted(value, axis, step, total):
    pairs = []
    for device in range(2**total):
        coords = box_coords(device, total)
        coords[axis] += step
        if 0 <= coords[axis] < 2 ** bit_counts(total)[axis]:
            pairs.append((device, box_index(coords, total)))
    return lax.ppermute(value, AXES, pairs)


def pieces(x):
    first = x.astype(BF16).astype(F32)
    rest = x - first
    second = rest.astype(BF16).astype(F32)
    third = (rest - second).astype(BF16).astype(F32)
    return first, second, third


def row_index(shape):
    return lax.broadcasted_iota(jnp.int32, shape, 0)


def placed(rows, offsets):
    eight = jnp.concatenate([rows, jnp.zeros_like(rows)], 0)
    index = row_index(eight.shape)
    shift = jnp.where(index == 0, offsets[0], jnp.where(index == 1, offsets[1], offsets[2]))
    return jnp.where(index < 3, eight + shift, 0.0)


def with_rows(base, extra):
    index = row_index(base.shape)
    for k, row in enumerate(extra):
        base = jnp.where(index == 3 + k, row, base)
    return base


def source_features(rows, offsets):
    x = placed(rows, offsets)
    high = x.astype(BF16).astype(F32)
    low = x - high
    norm = INVERSE * jnp.sum(x * x, axis=0, keepdims=True)
    ones = (1.0, 1.0, 1.0)
    groups = [with_rows(high, pieces(norm)), with_rows(high, ones), high, low, low, low]
    return jnp.concatenate(groups, 0)


def target_features(rows, offsets):
    x = placed(rows, offsets)
    w1, w2, w3 = pieces((-2.0 * INVERSE) * x)
    norm = INVERSE * (jnp.sum(x * x, axis=0, keepdims=True) + SOFTENING)
    ones = (1.0, 1.0, 1.0)
    return jnp.concatenate(
        [with_rows(w1, ones), with_rows(w2, pieces(norm)), w3, w1, w2, w3], 0
    )


def upward_kernel(counts, positions, charges, to_equiv, low, high, shape_out, equiv_out):
    n_points = positions.shape[2]
    n_chunks = n_points // CHUNK
    index = lax.broadcasted_iota(jnp.int32, (64, n_points), 0)
    surface = [
        ((index >> (2 * d)) & 3).astype(F32) * 0.5 - 0.25 for d in range(3)
    ]
    slot = lax.broadcasted_iota(jnp.int32, (32, n_points), 1)
    points = [positions[d].astype(F32) for d in range(3)]
    upward = []
    for leaf in range(8):
        out, at = (low, leaf) if leaf < 4 else (high, leaf - 4)
        count = counts[leaf]
        p = [points[d][leaf : leaf + 1] for d in range(3)]
        square = (surface[0] - p[0]) ** 2
        square = square + (surface[1] - p[1]) ** 2
        square = square + (surface[2] - p[2]) ** 2
        shape = (KERNEL_SCALE * lax.rsqrt(square + SOFTENING)).astype(BF16)
        shape_out[leaf] = shape
        q = jnp.where(slot < count, charges[leaf].astype(F32), 0.0).astype(BF16)
        upward.append(
            lax.dot_general(q, shape, (((1,), (1,)), ((), ())), preferred_element_type=F32)
        )
        live = lax.shift_right_logical(count + (CHUNK - 1), 7).astype(F32)
        rows = []
        for j in range(n_chunks):
            at_lanes = slice(CHUNK * j, CHUNK * (j + 1))
            out[at, 32 * j : 32 * j + 32, :] = q[:, at_lanes]
            rows += [row[:, at_lanes] for row in p]
            rows.append(jnp.full((1, CHUNK), live, F32))
        out[at, 128:144, :] = jnp.concatenate(rows, 0).astype(BF16)
    total = jnp.concatenate(upward, 0)
    equiv = jnp.zeros(total.shape, F32)
    for piece in pieces(total)[::-1]:
        equiv = equiv + jnp.dot(piece.astype(BF16), to_equiv[...], preferred_element_type=F32)
    equiv = equiv.astype(BF16)
    equiv_out[...] = jnp.concatenate([equiv[32 * l : 32 * l + 32] for l in range(8)], 1)


def targets_kernel(low, high, targets):
    for leaf in range(8):
        src, at = (low, leaf) if leaf < 4 else (high, leaf - 4)
        offsets = (leaf % 2 - 1.0, leaf // 2 % 2 - 1.0, leaf // 4 - 1.0)
        block = src[at, 128:144, :].astype(F32)
        for j in range(4):
            features = target_features(block[4 * j : 4 * j + 4], offsets)
            targets[4 * leaf + j] = features.T.astype(BF16)


def near_kernel(sides, with_before, leaves, sources, aims, *refs):
    payloads, refs = refs[: len(sides)], refs[len(sides) :]
    targets, refs = refs[0], refs[1:]
    if with_before:
        before, refs = refs[0], refs[1:]
    counts, out, features, values, live_v, live_s, queue, aim_queue, sem = refs
    n_leaves = sum(sides)
    n_tasks, n_sources = sources.shape
    n_aims = aims.shape[1]
    first = 0
    for payload, size in zip(payloads, sides):

        def one(leaf, _, payload=payload, first=first):
            block = payload[leaf, 128:144, :].astype(F32)
            at = first + leaf
            offsets = [leaves[at, d].astype(F32) for d in range(3)]
            for j in range(4):
                features[4 * at + j] = source_features(block[4 * j : 4 * j + 4], offsets).astype(
                    BF16
                )
                values[4 * at + j] = payload[leaf, 32 * j : 32 * j + 32, :]
            live_v[pl.ds(at, 1), :] = block[3:4].astype(jnp.int32)
            return 0

        lax.fori_loop(0, size, one, 0)
        first += size
    features[4 * n_leaves] = features[0]
    values[4 * n_leaves] = jnp.zeros((32, CHUNK), BF16)
    copy = pltpu.make_async_copy(live_v, live_s, sem)
    copy.start()
    copy.wait()
    out[...] = before[...] if with_before else jnp.zeros_like(out)

    def compute(start, n_rows, n_items):
        places = [aim_queue[start + i] for i in range(n_rows)]
        rows = jnp.concatenate([targets[place] for place in places], 0)

        def add(at, width, total):
            items = [queue[at + k] for k in range(width)]
            u = jnp.concatenate([features[item] for item in items], 1)
            q = jnp.concatenate([values[item] for item in items], 1)
            square = jnp.dot(rows, u, preferred_element_type=F32)
            kern = lax.rsqrt(square).astype(BF16)
            return total + lax.dot_general(
                q, kern, (((1,), (1,)), ((), ())), preferred_element_type=F32
            )

        def store(total):
            for i, place in enumerate(places):
                out[place] += total[:, CHUNK * i : CHUNK * (i + 1)]

        full = n_items // 12
        rest = n_items - 12 * full
        total = lax.fori_loop(
            0, full, lambda c, t: add(12 * c, 12, t), jnp.zeros((32, CHUNK * n_rows), F32)
        )
        store(total)
        for width in (4, 8, 12):

            @pl.when((rest > width - 4) & (rest <= width))
            def _(width=width):
                store(add(12 * full, width, jnp.zeros((32, CHUNK * n_rows), F32)))

    def task(i, _):
        n_items = jnp.int32(0)
        for k in range(n_sources):
            leaf = sources[i, k]
            n_live = jnp.where(leaf >= 0, live_s[jnp.maximum(leaf, 0), 0], 0)
            for j in range(4):
                queue[n_items] = 4 * leaf + j
                n_items = n_items + (j < n_live).astype(jnp.int32)
        for k in range(12):
            queue[n_items + k] = 4 * n_leaves
        n_rows = jnp.int32(0)
        for k in range(n_aims):
            leaf = aims[i, k]
            count = jnp.where(leaf >= 0, counts[jnp.maximum(leaf, 0)], 0)
            for j in range(4):
                aim_queue[n_rows] = 4 * leaf + j
                n_rows = n_rows + (CHUNK * j < count).astype(jnp.int32)

        @pl.when(n_items > 0)
        def _():
            full = n_rows // 4

            def four(c, _):
                compute(4 * c, 4, n_items)
                return 0

            lax.fori_loop(0, full, four, 0)
            for rest in (1, 2, 3):

                @pl.when(n_rows - 4 * full == rest)
                def _(rest=rest):
                    compute(4 * full, rest, n_items)

        return 0

    lax.fori_loop(0, n_tasks, task, 0)


def faces_kernel(x_low, z_low, low, high, z_high, x_high, *faces):
    for y in range(2):
        for z, plane in enumerate((z_low, low, high, z_high)):
            faces[y][4 * z] = x_low[2 * z + y]
            faces[y][4 * z + 1] = plane[2 * y]
            faces[y][4 * z + 2] = plane[2 * y + 1]
            faces[y][4 * z + 3] = x_high[2 * z + y]


def widen_kernel(table, wide, rows):
    n_equiv = table.shape[0]
    window = 6 * n_equiv
    n_offsets = table.shape[2]
    n_lanes = 3 * CHUNK
    stride = n_equiv + 1
    together = 8
    unit = row_index((CHUNK, CHUNK)) == lax.broadcasted_iota(jnp.int32, (CHUNK, CHUNK), 1)
    unit = jnp.where(unit, 1.0, 0.0).astype(BF16)

    def turn(i, _):
        parts = []
        for m in range(together):
            x = jnp.concatenate(
                [
                    table[together * i + m].astype(F32),
                    jnp.zeros((n_equiv, n_lanes - n_offsets), F32),
                ],
                1,
            )
            parts += [pltpu.roll(x, n_lanes - 1, 1), x]
        both = jnp.concatenate(parts, 0).astype(BF16)
        for c in range(n_lanes // CHUNK):
            turned = lax.dot_general(
                unit,
                both[:, CHUNK * c : CHUNK * (c + 1)],
                (((1,), (1,)), ((), ())),
                preferred_element_type=F32,
            )
            for m in range(together):
                at = pl.ds(CHUNK * c * stride + together * i + m, CHUNK, stride=stride)
                rows[at, :] = turned[:, CHUNK * m : CHUNK * (m + 1)]
        return 0

    lax.fori_loop(0, n_equiv // together, turn, 0)
    index = lax.broadcasted_iota(jnp.int32, (window, 2 * n_equiv), 0)
    lane = lax.broadcasted_iota(jnp.int32, (window, 2 * n_equiv), 1)
    first = jnp.where(lane < n_equiv, n_equiv, 2 * n_equiv)
    beside = (index >= first) & (index < first + 3 * n_equiv)

    def pack(i, _):
        oz, oy = i // 7, i % 7
        near = (jnp.abs(oz - 3) <= 1) & (jnp.abs(oy - 3) <= 1)
        block = jnp.concatenate(
            [rows[pl.ds((7 * i + x) * stride, n_equiv), :] for x in range(6)], 0
        )
        block = jnp.where(near & beside, 0.0, block)
        wide[oz, pl.ds(pl.multiple_of(oy * window, window), window), :] = block.astype(BF16)
        return 0

    lax.fori_loop(0, 49, pack, 0)


def far_kernel(
    total_bits,
    counts,
    gathered_hbm,
    wide_hbm,
    up,
    down,
    shape,
    near,
    out,
    gathered,
    wide,
    boxes,
    region,
    sems,
):
    n_equiv = 64
    window = 6 * n_equiv
    bits = bit_counts(total_bits)
    n_pairs = gathered.shape[0]
    step = n_pairs // 4
    copies = []
    for i in range(4):
        part = pl.ds(step * i, step)
        copies.append(pltpu.make_async_copy(gathered_hbm.at[part], gathered.at[part], sems.at[i]))
    copies.append(pltpu.make_async_copy(wide_hbm, wide, sems.at[4]))
    for copy in copies:
        copy.start()
    me = lax.axis_index("oct") * lax.axis_size("leaf") + lax.axis_index("leaf")
    cx, cy, cz = box_coords(me, total_bits)
    zeros_up = jnp.zeros((8 * n_equiv, n_equiv), F32)
    up_rows = up[...].astype(F32).reshape(8 * n_equiv, n_equiv)
    up_even = jnp.concatenate([up_rows, zeros_up], 1).astype(BF16)
    up_odd = jnp.concatenate([zeros_up, up_rows], 1).astype(BF16)
    for i in range(4):
        copies[i].wait()
        at = slice(step * i, step * (i + 1))
        even = gathered[at, 0].reshape(step * 32, 8 * n_equiv)
        odd = gathered[at, 1].reshape(step * 32, 8 * n_equiv)
        both = jnp.dot(even, up_even, preferred_element_type=F32)
        both = both + jnp.dot(odd, up_odd, preferred_element_type=F32)
        boxes[at] = both.astype(BF16).reshape(step, 32, 2 * n_equiv)

    region[0] = jnp.zeros_like(region[0])
    region[7] = jnp.zeros_like(region[7])
    for bz in range(3):
        for by in range(3):
            for bx in range(3):
                z, y, x = cz + bz - 1, cy + by - 1, cx + bx - 1
                inside = (
                    (z >= 0)
                    & (z < 2 ** bits[2])
                    & (y >= 0)
                    & (y < 2 ** bits[1])
                    & (x >= 0)
                    & (x < 2 ** bits[0])
                )
                box = jnp.where(inside, box_index([x, y, z], total_bits), 0)
                data = gathered[box >> 1, box & 1]
                data = jnp.where(inside, data, jnp.zeros_like(data))
                for lz in range(2):
                    for ly in range(2):
                        at = (2 * by + ly) * window + bx * 2 * n_equiv
                        part = (2 * lz + ly) * 2 * n_equiv
                        region[1 + 2 * bz + lz, :, at : at + 2 * n_equiv] = data[
                            :, part : part + 2 * n_equiv
                        ]

    copies[4].wait()

    parent = cx >> 1
    total = jnp.zeros((32, 2 * n_equiv), F32)
    zero = jnp.zeros((32, 2 * n_equiv), BF16)
    span_y = 2 ** bits[1]
    for z in range(2 ** bits[2]):
        row = []
        for y in range(span_y):
            for dx in (-1, 0, 1):
                px = parent + dx
                inside = (px >= 0) & (px < 2 ** (bits[0] - 1))
                pair = box_index([2 * jnp.where(inside, px, 0), y, z], total_bits) >> 1
                row.append(jnp.where(inside, boxes[pair], zero))
        start = pl.multiple_of((3 - cy) * window, window)
        right = wide[z - cz + 3, pl.ds(start, span_y * window), :]
        total = total + jnp.dot(jnp.concatenate(row, 1), right, preferred_element_type=F32)
    total = jnp.where((cx & 1) == 0, total, pltpu.roll(total, n_equiv, 1))
    box_local = (0.5 * total[:, :n_equiv]).astype(BF16)
    down_row = jnp.concatenate([down[l] for l in range(8)], 1)
    inherited = jnp.dot(box_local, down_row, preferred_element_type=F32)

    sums = [jnp.zeros((64, 2 * n_equiv), F32) for _ in range(2)]
    for a in range(7):
        left = region[a : a + 2].reshape(64, 6 * window)
        for ty in range(2):
            right = wide[a, (1 - ty) * window : (7 - ty) * window, :]
            sums[ty] = sums[ty] + jnp.dot(left, right, preferred_element_type=F32)
    n_points = out.shape[2]
    slot = lax.broadcasted_iota(jnp.int32, (32, n_points), 1)
    lane = lax.broadcasted_iota(jnp.int32, (32, 2 * n_equiv), 1)
    for tz in range(2):
        for ty in range(2):
            first = 4 * tz + 2 * ty
            local = (
                inherited[:, first * n_equiv : (first + 2) * n_equiv]
                + sums[ty][32 * tz : 32 * tz + 32]
            )
            left = jnp.concatenate(
                [jnp.where(lane < n_equiv, local, 0.0), jnp.where(lane < n_equiv, 0.0, local)], 0
            ).astype(BF16)
            right = shape[first : first + 2].reshape(2 * n_equiv, n_points)
            far = jnp.dot(left, right, preferred_element_type=F32)
            for tx in range(2):
                value = jnp.concatenate([near[4 * (first + tx) + j] for j in range(4)], 1)
                value = value + far[32 * tx : 32 * tx + 32]
                out[first + tx] = jnp.where(slot < counts[first + tx], value, 0.0)


def call(kernel, ins, outs, scratch=(), flops=0, seen=0, limit=28, **kwargs):
    return pl.pallas_call(
        kernel,
        out_shape=outs,
        in_specs=ins,
        out_specs=jax.tree.map(lambda _: VMEM, outs),
        scratch_shapes=list(scratch),
        compiler_params=pltpu.CompilerParams(vmem_limit_bytes=limit * MIB),
        cost_estimate=pl.CostEstimate(flops=flops, bytes_accessed=seen, transcendentals=0),
        **kwargs,
    )


def near_tables():
    both = range(2)
    own = [(x, y, z) for z in (1, 2) for y in (1, 2) for x in (1, 2)]
    z_side = [(x, y, 3 * side) for side in both for y in (1, 2) for x in (1, 2)]
    x_side = [(3 * side, y, z) for side in both for z in range(4) for y in (1, 2)]
    y_side = [(x, 3 * side, z) for side in both for z in range(4) for x in range(4)]
    eight = list(range(8))
    middle = []
    for side in both:
        four = [4 * side + i for i in range(4)]
        middle.append((four, four))
    for tx in both:
        for tz in both:
            six = [8 + 8 * tx + 2 * tz + i for i in range(6)]
            middle.append((six, [4 * tz + 2 * ty + tx for ty in both]))
    last = []
    for ty in both:
        for tz in both:
            for tx in both:
                nine = [
                    16 * ty + 4 * (tz + dz) + tx + dx for dz in range(3) for dx in range(3)
                ]
                last.append((nine, [4 * tz + 2 * ty + tx]))
    return {
        "first": ((4, 4), own, [(eight, [0, 1, 2, 3])]),
        "second": ((4, 4), own, [(eight, [4, 5, 6, 7])]),
        "middle": ((4, 4, 8, 8), z_side + x_side, middle),
        "last": ((16, 16), y_side, last),
    }


def near_call(phase, payloads, targets, counts, before):
    sides, places, tasks = near_tables()[phase]
    n_leaves = sum(sides)
    n_sources = max(len(task[0]) for task in tasks)
    n_aims = max(len(task[1]) for task in tasks)
    pad = lambda row, size: row + [-1] * (size - len(row))
    tables = [
        np.array(places, np.int32) - 2,
        np.array([pad(task[0], n_sources) for task in tasks], np.int32),
        np.array([pad(task[1], n_aims) for task in tasks], np.int32),
    ]
    args = [jnp.asarray(table) for table in tables] + list(payloads) + [targets]
    if before is not None:
        args.append(before)
    args.append(counts)
    us = {"first": 12, "second": 12, "middle": 25, "last": 15}[phase]
    return call(
        functools.partial(near_kernel, sides, before is not None),
        [SMEM] * 3 + [VMEM] * (len(args) - 4) + [SMEM],
        jax.ShapeDtypeStruct((32, 32, CHUNK), F32),
        [
            pltpu.VMEM((4 * n_leaves + 1, FEATURES, CHUNK), BF16),
            pltpu.VMEM((4 * n_leaves + 1, 32, CHUNK), BF16),
            pltpu.VMEM((n_leaves, CHUNK), jnp.int32),
            pltpu.SMEM((n_leaves, CHUNK), jnp.int32),
            pltpu.SMEM((64,), jnp.int32),
            pltpu.SMEM((40,), jnp.int32),
            pltpu.SemaphoreType.DMA,
        ],
        flops=us * 10**9,
        seen=us * 10**6,
        name="near_" + phase,
    )(*args)


def per_device(positions, charges, counts, check_to_equiv, up_child, down_child, translate):
    n_points = positions.shape[2]
    n_probe = charges.shape[1]
    n_devices = lax.axis_size(AXES)
    total_bits = n_devices.bit_length() - 1
    shape_of = jax.ShapeDtypeStruct
    half = shape_of((4, ROWS, CHUNK), BF16)
    low, high, shape, equiv = call(
        upward_kernel,
        [SMEM, VMEM, VMEM, VMEM],
        (half, half, shape_of((8, 64, n_points), BF16), shape_of((n_probe, 512), BF16)),
        seen=3 * 10**6,
        flops=3 * 10**9,
        limit=56,
        name="upward",
    )(counts, positions.transpose(1, 0, 2), charges, check_to_equiv)
    move = functools.partial(shifted, total=total_bits)
    z_low = move(high, 2, 1)
    z_high = move(low, 2, -1)
    gathered = lax.all_gather(equiv, AXES, axis=0)
    targets = call(
        targets_kernel,
        [VMEM] * 2,
        shape_of((32, CHUNK, FEATURES), BF16),
        seen=10**6,
        flops=10**9,
        name="targets",
    )(low, high)
    near = near_call("first", (low, high), targets, counts, None)
    z_low, z_high, near = lax.optimization_barrier((z_low, z_high, near))
    planes = [a.reshape(2, 2, ROWS, CHUNK) for a in (z_low, low, high, z_high)]
    faces = [jnp.stack([a[:, x] for a in planes]).reshape(8, ROWS, CHUNK) for x in range(2)]
    faces[0], faces[1], near = lax.optimization_barrier((faces[0], faces[1], near))
    x_low = move(faces[1], 0, 1)
    x_high = move(faces[0], 0, -1)
    near = near_call("second", (low, high), targets, counts, near)
    x_low, x_high, near = lax.optimization_barrier((x_low, x_high, near))
    plane = shape_of((16, ROWS, CHUNK), BF16)
    y_faces = call(
        faces_kernel, [VMEM] * 6, (plane, plane), seen=3 * 10**6, flops=10**9, name="faces"
    )(x_low, z_low, low, high, z_high, x_high)
    face_0, face_1, near = lax.optimization_barrier((*y_faces, near))
    y_low = move(face_1, 1, 1)
    y_high = move(face_0, 1, -1)
    near = near_call("middle", (z_low, z_high, x_low, x_high), targets, counts, near)
    translate, near = lax.optimization_barrier((translate, near))
    wide = call(
        widen_kernel,
        [VMEM],
        shape_of((7, 7 * 6 * 64, 128), BF16),
        [pltpu.VMEM((3 * CHUNK * 65, 128), F32)],
        limit=56,
        seen=6 * 10**6,
        flops=6 * 10**9,
        name="widen",
    )(translate.transpose(1, 2, 0))
    wide, near, y_low, y_high = lax.optimization_barrier((wide, near, y_low, y_high))
    near = near_call("last", (y_low, y_high), targets, counts, near)
    anywhere = pl.BlockSpec(memory_space=pl.ANY)
    return call(
        functools.partial(far_kernel, total_bits),
        [SMEM, anywhere, anywhere] + [VMEM] * 4,
        shape_of((8, n_probe, n_points), F32),
        [
            pltpu.VMEM((n_devices // 2, 2, n_probe, 512), BF16),
            pltpu.VMEM((7, 7 * 6 * 64, 128), BF16),
            pltpu.VMEM((n_devices // 2, n_probe, 128), BF16),
            pltpu.VMEM((8, n_probe, 36 * 64), BF16),
            pltpu.SemaphoreType.DMA((5,)),
        ],
        seen=10 * 10**6,
        flops=8 * 10**9,
        limit=56,
        name="far",
    )(
        counts,
        gathered.reshape(n_devices // 2, 2, n_probe, 512),
        wide,
        up_child,
        down_child,
        shape,
        near,
    )


def solution(mesh):
    split = P(AXES, None, None)
    return jax.shard_map(
        per_device,
        mesh=mesh,
        in_specs=(split, split, P(AXES), P(), P(), P(), P()),
        out_specs=split,
        check_vma=False,
    )
```

```python
import functools

import jax
import jax.numpy as jnp
from jax import lax
from jax.experimental import pallas as pl
from jax.experimental.pallas import tpu as pltpu
from jax.sharding import PartitionSpec as P

AXES = ("oct", "leaf")
KERNEL_SCALE = 0.02
SOFTENING = 0.01
INVERSE = 1.0 / KERNEL_SCALE**2
CHUNK = 128
ROWS = 144
FEATURES = 48
MIB = 1 << 20
F32 = jnp.float32
BF16 = jnp.bfloat16
VMEM = pl.BlockSpec(memory_space=pltpu.VMEM)
SMEM = pl.BlockSpec(memory_space=pltpu.SMEM)


def bit_counts(total):
    return [(total + 2) // 3, (total + 1) // 3, total // 3]


def box_coords(index, total):
    coords = []
    for j, bits in enumerate(bit_counts(total)):
        value = 0
        for k in range(bits):
            value = value + ((index >> (3 * k + j)) & 1) * 2**k
        coords.append(value)
    return coords


def box_index(coords, total):
    index = 0
    for j, bits in enumerate(bit_counts(total)):
        for k in range(bits):
            index = index + ((coords[j] >> k) & 1) * 2 ** (3 * k + j)
    return index


def shifted(value, axis, step, total):
    pairs = []
    for device in range(2**total):
        coords = box_coords(device, total)
        coords[axis] += step
        if 0 <= coords[axis] < 2 ** bit_counts(total)[axis]:
            pairs.append((device, box_index(coords, total)))
    return lax.ppermute(value, AXES, pairs)


def pieces(x):
    first = x.astype(BF16).astype(F32)
    rest = x - first
    second = rest.astype(BF16).astype(F32)
    third = (rest - second).astype(BF16).astype(F32)
    return first, second, third


def row_index(shape):
    return lax.broadcasted_iota(jnp.int32, shape, 0)


def placed(rows, offsets):
    eight = jnp.concatenate([rows, jnp.zeros_like(rows)], 0)
    index = row_index(eight.shape)
    shift = jnp.where(index == 0, offsets[0], jnp.where(index == 1, offsets[1], offsets[2]))
    return jnp.where(index < 3, eight + shift, 0.0)


def with_rows(base, extra):
    index = row_index(base.shape)
    for k, row in enumerate(extra):
        base = jnp.where(index == 3 + k, row, base)
    return base


def source_features(rows, offsets):
    x = placed(rows, offsets)
    high = x.astype(BF16).astype(F32)
    low = x - high
    norm = INVERSE * jnp.sum(x * x, axis=0, keepdims=True)
    ones = (1.0, 1.0, 1.0)
    groups = [with_rows(high, pieces(norm)), with_rows(high, ones), high, low, low, low]
    return jnp.concatenate(groups, 0)


def target_features(rows, offsets):
    x = placed(rows, offsets)
    w1, w2, w3 = pieces((-2.0 * INVERSE) * x)
    norm = INVERSE * (jnp.sum(x * x, axis=0, keepdims=True) + SOFTENING)
    ones = (1.0, 1.0, 1.0)
    return jnp.concatenate(
        [with_rows(w1, ones), with_rows(w2, pieces(norm)), w3, w1, w2, w3], 0
    )


def upward_kernel(counts, positions, charges, to_equiv, low, high, shape_out, equiv_out):
    n_points = positions.shape[2]
    n_chunks = n_points // CHUNK
    index = lax.broadcasted_iota(jnp.int32, (64, n_points), 0)
    surface = [
        ((index >> (2 * d)) & 3).astype(F32) * 0.5 - 0.25 for d in range(3)
    ]
    slot = lax.broadcasted_iota(jnp.int32, (32, n_points), 1)
    points = [positions[d].astype(F32) for d in range(3)]
    upward = []
    for leaf in range(8):
        out, at = (low, leaf) if leaf < 4 else (high, leaf - 4)
        count = counts[leaf]
        p = [points[d][leaf : leaf + 1] for d in range(3)]
        square = (surface[0] - p[0]) ** 2
        square = square + (surface[1] - p[1]) ** 2
        square = square + (surface[2] - p[2]) ** 2
        shape = (KERNEL_SCALE * lax.rsqrt(square + SOFTENING)).astype(BF16)
        shape_out[leaf] = shape
        q = jnp.where(slot < count, charges[leaf].astype(F32), 0.0).astype(BF16)
        upward.append(
            lax.dot_general(q, shape, (((1,), (1,)), ((), ())), preferred_element_type=F32)
        )
        live = lax.shift_right_logical(count + (CHUNK - 1), 7).astype(F32)
        rows = []
        for j in range(n_chunks):
            at_lanes = slice(CHUNK * j, CHUNK * (j + 1))
            out[at, 32 * j : 32 * j + 32, :] = q[:, at_lanes]
            rows += [row[:, at_lanes] for row in p]
            rows.append(jnp.full((1, CHUNK), live, F32))
        out[at, 128:144, :] = jnp.concatenate(rows, 0).astype(BF16)
    total = jnp.concatenate(upward, 0)
    equiv = jnp.zeros(total.shape, F32)
    for piece in pieces(total)[::-1]:
        equiv = equiv + jnp.dot(piece.astype(BF16), to_equiv[...], preferred_element_type=F32)
    equiv = equiv.astype(BF16)
    equiv_out[...] = jnp.concatenate([equiv[32 * l : 32 * l + 32] for l in range(8)], 1)


def near_kernel(sides, opens, tables, *refs):
    payloads, refs = refs[: len(sides)], refs[len(sides) :]
    if opens:
        counts, out, targets, low, high, *refs = refs
    else:
        targets, before, counts, out, *refs = refs
    features, values, live_v, live_s, queue, aim_queue, leaves, sources, aims = refs
    for table, ref in zip(tables, (leaves, sources, aims)):
        for i, row in enumerate(table):
            for k, entry in enumerate(row):
                ref[i, k] = jnp.int32(entry)
    n_leaves = sum(sides)
    n_tasks, n_sources = sources.shape
    n_aims = aims.shape[1]
    first = 0
    for payload, size in zip(payloads, sides):

        def one(leaf, _, payload=payload, first=first):
            block = payload[leaf, 128:144, :].astype(F32)
            at = first + leaf
            offsets = [leaves[at, d].astype(F32) for d in range(3)]
            for j in range(4):
                features[4 * at + j] = source_features(block[4 * j : 4 * j + 4], offsets).astype(
                    BF16
                )
                values[4 * at + j] = payload[leaf, 32 * j : 32 * j + 32, :]
            live_v[pl.ds(at, 1), :] = block[3:4].astype(jnp.int32)
            return 0

        lax.fori_loop(0, size, one, 0)
        first += size
    features[4 * n_leaves] = features[0]
    values[4 * n_leaves] = jnp.zeros((32, CHUNK), BF16)
    for at in range(n_leaves):
        live_s[at] = live_v[at : at + 1, :][0, 0]
    if opens:
        out[...] = jnp.zeros_like(out)
        low[...] = payloads[0][...]
        high[...] = payloads[1][...]
        for leaf in range(8):
            block = payloads[leaf // 4][leaf % 4, 128:144, :].astype(F32)
            offsets = (leaf % 2 - 1.0, leaf // 2 % 2 - 1.0, leaf // 4 - 1.0)
            for j in range(4):
                rows = target_features(block[4 * j : 4 * j + 4], offsets)
                targets[4 * leaf + j] = rows.T.astype(BF16)
    else:
        out[...] = before[...]

    def compute(start, n_rows, n_items):
        places = [aim_queue[start + i] for i in range(n_rows)]
        rows = jnp.concatenate([targets[place] for place in places], 0)

        def add(at, width, total):
            items = [queue[at + k] for k in range(width)]
            u = jnp.concatenate([features[item] for item in items], 1)
            q = jnp.concatenate([values[item] for item in items], 1)
            square = jnp.dot(rows, u, preferred_element_type=F32)
            kern = lax.rsqrt(square).astype(BF16)
            return total + lax.dot_general(
                q, kern, (((1,), (1,)), ((), ())), preferred_element_type=F32
            )

        def store(total):
            for i, place in enumerate(places):
                out[place] += total[:, CHUNK * i : CHUNK * (i + 1)]

        full = n_items // 12
        rest = n_items - 12 * full
        total = lax.fori_loop(
            0, full, lambda c, t: add(12 * c, 12, t), jnp.zeros((32, CHUNK * n_rows), F32)
        )
        store(total)
        for width in (4, 8, 12):

            @pl.when((rest > width - 4) & (rest <= width))
            def _(width=width):
                store(add(12 * full, width, jnp.zeros((32, CHUNK * n_rows), F32)))

    def task(i, _):
        n_items = jnp.int32(0)
        for k in range(n_sources):
            leaf = sources[i, k]
            n_live = jnp.where(leaf >= 0, live_s[jnp.maximum(leaf, 0)], 0)
            for j in range(4):
                queue[n_items] = 4 * leaf + j
                n_items = n_items + (j < n_live).astype(jnp.int32)
        for k in range(12):
            queue[n_items + k] = 4 * n_leaves
        n_rows = jnp.int32(0)
        for k in range(n_aims):
            leaf = aims[i, k]
            count = jnp.where(leaf >= 0, counts[jnp.maximum(leaf, 0)], 0)
            for j in range(4):
                aim_queue[n_rows] = 4 * leaf + j
                n_rows = n_rows + (CHUNK * j < count).astype(jnp.int32)

        @pl.when(n_items > 0)
        def _():
            full = n_rows // 4

            def four(c, _):
                compute(4 * c, 4, n_items)
                return 0

            lax.fori_loop(0, full, four, 0)
            for rest in (1, 2, 3):

                @pl.when(n_rows - 4 * full == rest)
                def _(rest=rest):
                    compute(4 * full, rest, n_items)

        return 0

    lax.fori_loop(0, n_tasks, task, 0)


def faces_kernel(x_low, z_low, low, high, z_high, x_high, *faces):
    for y in range(2):
        for z, plane in enumerate((z_low, low, high, z_high)):
            faces[y][4 * z] = x_low[2 * z + y]
            faces[y][4 * z + 1] = plane[2 * y]
            faces[y][4 * z + 2] = plane[2 * y + 1]
            faces[y][4 * z + 3] = x_high[2 * z + y]


def widen_kernel(table, wide, rows):
    n_equiv = table.shape[0]
    window = 6 * n_equiv
    n_offsets = table.shape[2]
    n_lanes = 3 * CHUNK
    stride = n_equiv + 1
    together = 16
    unit = row_index((CHUNK, CHUNK)) == lax.broadcasted_iota(jnp.int32, (CHUNK, CHUNK), 1)
    unit = jnp.where(unit, 1.0, 0.0).astype(BF16)

    def turn(i, _):
        parts = []
        for m in range(together):
            x = jnp.concatenate(
                [
                    table[together * i + m].astype(F32),
                    jnp.zeros((n_equiv, n_lanes - n_offsets), F32),
                ],
                1,
            )
            parts += [pltpu.roll(x, n_lanes - 1, 1), x]
        both = jnp.concatenate(parts, 0).astype(BF16)
        for c in range(n_lanes // CHUNK):
            turned = lax.dot_general(
                unit,
                both[:, CHUNK * c : CHUNK * (c + 1)],
                (((1,), (1,)), ((), ())),
                preferred_element_type=F32,
            )
            for m in range(together):
                at = pl.ds(CHUNK * c * stride + together * i + m, CHUNK, stride=stride)
                rows[at, :] = turned[:, CHUNK * m : CHUNK * (m + 1)]
        return 0

    lax.fori_loop(0, n_equiv // together, turn, 0)
    index = lax.broadcasted_iota(jnp.int32, (window, 2 * n_equiv), 0)
    lane = lax.broadcasted_iota(jnp.int32, (window, 2 * n_equiv), 1)
    first = jnp.where(lane < n_equiv, n_equiv, 2 * n_equiv)
    beside = (index >= first) & (index < first + 3 * n_equiv)

    def pack(i, _):
        oz, oy = i // 7, i % 7
        near = (jnp.abs(oz - 3) <= 1) & (jnp.abs(oy - 3) <= 1)
        block = jnp.concatenate(
            [rows[pl.ds((7 * i + x) * stride, n_equiv), :] for x in range(6)], 0
        )
        block = jnp.where(near & beside, 0.0, block)
        wide[oz, pl.ds(pl.multiple_of(oy * window, window), window), :] = block.astype(BF16)
        return 0

    lax.fori_loop(0, 49, pack, 0)


def far_kernel(
    total_bits,
    counts,
    gathered_hbm,
    wide_hbm,
    up,
    down,
    shape,
    near,
    out,
    gathered,
    wide,
    boxes,
    region,
    sems,
):
    n_equiv = 64
    window = 6 * n_equiv
    bits = bit_counts(total_bits)
    n_pairs = gathered.shape[0]
    step = n_pairs // 4
    copies = []
    for i in range(4):
        part = pl.ds(step * i, step)
        copies.append(pltpu.make_async_copy(gathered_hbm.at[part], gathered.at[part], sems.at[i]))
    copies.append(pltpu.make_async_copy(wide_hbm, wide, sems.at[4]))
    for copy in copies:
        copy.start()
    me = lax.axis_index("oct") * lax.axis_size("leaf") + lax.axis_index("leaf")
    cx, cy, cz = box_coords(me, total_bits)
    zeros_up = jnp.zeros((8 * n_equiv, n_equiv), F32)
    up_rows = up[...].astype(F32).reshape(8 * n_equiv, n_equiv)
    up_even = jnp.concatenate([up_rows, zeros_up], 1).astype(BF16)
    up_odd = jnp.concatenate([zeros_up, up_rows], 1).astype(BF16)
    for i in range(4):
        copies[i].wait()
        at = slice(step * i, step * (i + 1))
        even = gathered[at, 0].reshape(step * 32, 8 * n_equiv)
        odd = gathered[at, 1].reshape(step * 32, 8 * n_equiv)
        both = jnp.dot(even, up_even, preferred_element_type=F32)
        both = both + jnp.dot(odd, up_odd, preferred_element_type=F32)
        boxes[at] = both.astype(BF16).reshape(step, 32, 2 * n_equiv)

    region[0] = jnp.zeros_like(region[0])
    region[7] = jnp.zeros_like(region[7])
    for bz in range(3):
        for by in range(3):
            for bx in range(3):
                z, y, x = cz + bz - 1, cy + by - 1, cx + bx - 1
                inside = (
                    (z >= 0)
                    & (z < 2 ** bits[2])
                    & (y >= 0)
                    & (y < 2 ** bits[1])
                    & (x >= 0)
                    & (x < 2 ** bits[0])
                )
                box = jnp.where(inside, box_index([x, y, z], total_bits), 0)
                data = gathered[box >> 1, box & 1]
                data = jnp.where(inside, data, jnp.zeros_like(data))
                for lz in range(2):
                    for ly in range(2):
                        at = (2 * by + ly) * window + bx * 2 * n_equiv
                        part = (2 * lz + ly) * 2 * n_equiv
                        region[1 + 2 * bz + lz, :, at : at + 2 * n_equiv] = data[
                            :, part : part + 2 * n_equiv
                        ]

    copies[4].wait()

    parent = cx >> 1
    total = jnp.zeros((32, 2 * n_equiv), F32)
    zero = jnp.zeros((32, 2 * n_equiv), BF16)
    span_y = 2 ** bits[1]
    for z in range(2 ** bits[2]):
        row = []
        for y in range(span_y):
            for dx in (-1, 0, 1):
                px = parent + dx
                inside = (px >= 0) & (px < 2 ** (bits[0] - 1))
                pair = box_index([2 * jnp.where(inside, px, 0), y, z], total_bits) >> 1
                row.append(jnp.where(inside, boxes[pair], zero))
        start = pl.multiple_of((3 - cy) * window, window)
        right = wide[z - cz + 3, pl.ds(start, span_y * window), :]
        total = total + jnp.dot(jnp.concatenate(row, 1), right, preferred_element_type=F32)
    total = jnp.where((cx & 1) == 0, total, pltpu.roll(total, n_equiv, 1))
    box_local = (0.5 * total[:, :n_equiv]).astype(BF16)
    down_row = jnp.concatenate([down[l] for l in range(8)], 1)
    inherited = jnp.dot(box_local, down_row, preferred_element_type=F32)

    sums = [jnp.zeros((64, 2 * n_equiv), F32) for _ in range(2)]
    for a in range(7):
        left = region[a : a + 2].reshape(64, 6 * window)
        for ty in range(2):
            right = wide[a, (1 - ty) * window : (7 - ty) * window, :]
            sums[ty] = sums[ty] + jnp.dot(left, right, preferred_element_type=F32)
    n_points = out.shape[2]
    slot = lax.broadcasted_iota(jnp.int32, (32, n_points), 1)
    lane = lax.broadcasted_iota(jnp.int32, (32, 2 * n_equiv), 1)
    for tz in range(2):
        for ty in range(2):
            first = 4 * tz + 2 * ty
            local = (
                inherited[:, first * n_equiv : (first + 2) * n_equiv]
                + sums[ty][32 * tz : 32 * tz + 32]
            )
            left = jnp.concatenate(
                [jnp.where(lane < n_equiv, local, 0.0), jnp.where(lane < n_equiv, 0.0, local)], 0
            ).astype(BF16)
            right = shape[first : first + 2].reshape(2 * n_equiv, n_points)
            far = jnp.dot(left, right, preferred_element_type=F32)
            for tx in range(2):
                value = jnp.concatenate([near[4 * (first + tx) + j] for j in range(4)], 1)
                value = value + far[32 * tx : 32 * tx + 32]
                out[first + tx] = jnp.where(slot < counts[first + tx], value, 0.0)


def call(kernel, ins, outs, scratch=(), flops=0, seen=0, limit=28, **kwargs):
    return pl.pallas_call(
        kernel,
        out_shape=outs,
        in_specs=ins,
        out_specs=jax.tree.map(lambda _: VMEM, outs),
        scratch_shapes=list(scratch),
        compiler_params=pltpu.CompilerParams(vmem_limit_bytes=limit * MIB),
        cost_estimate=pl.CostEstimate(flops=flops, bytes_accessed=seen, transcendentals=0),
        **kwargs,
    )


def near_tables():
    both = range(2)
    own = [(x, y, z) for z in (1, 2) for y in (1, 2) for x in (1, 2)]
    z_side = [(x, y, 3 * side) for side in both for y in (1, 2) for x in (1, 2)]
    x_side = [(3 * side, y, z) for side in both for z in range(4) for y in (1, 2)]
    y_side = [(x, 3 * side, z) for side in both for z in range(4) for x in range(4)]
    eight = list(range(8))
    middle = []
    for side in both:
        four = [4 * side + i for i in range(4)]
        middle.append((four, four))
    for tx in both:
        for tz in both:
            six = [8 + 8 * tx + 2 * tz + i for i in range(6)]
            middle.append((six, [4 * tz + 2 * ty + tx for ty in both]))
    last = []
    for ty in both:
        for tz in both:
            for tx in both:
                nine = [
                    16 * ty + 4 * (tz + dz) + tx + dx for dz in range(3) for dx in range(3)
                ]
                last.append((nine, [4 * tz + 2 * ty + tx]))
    return {
        "first": ((4, 4), own, [(eight, [0, 1, 2, 3])]),
        "second": ((4, 4), own, [(eight, [4, 5, 6, 7])]),
        "middle": ((4, 4, 8, 8), z_side + x_side, middle),
        "last": ((16, 16), y_side, last),
    }


def near_call(phase, payloads, targets, counts, before):
    sides, places, tasks = near_tables()[phase]
    n_leaves = sum(sides)
    n_sources = max(len(task[0]) for task in tasks)
    n_aims = max(len(task[1]) for task in tasks)
    pad = lambda row, size: row + [-1] * (size - len(row))
    tables = [
        [[c - 2 for c in place] for place in places],
        [pad(task[0], n_sources) for task in tasks],
        [pad(task[1], n_aims) for task in tasks],
    ]
    opens = before is None
    args = list(payloads)
    outs = jax.ShapeDtypeStruct((32, 32, CHUNK), F32)
    if opens:
        half = jax.ShapeDtypeStruct(payloads[0].shape, BF16)
        outs = (outs, jax.ShapeDtypeStruct((32, CHUNK, FEATURES), BF16), half, half)
    else:
        args += [targets, before]
    args.append(counts)
    us = {"first": 12, "second": 12, "middle": 25, "last": 15}[phase]
    return call(
        functools.partial(near_kernel, sides, opens, tables),
        [VMEM] * (len(args) - 1) + [SMEM],
        outs,
        [
            pltpu.VMEM((4 * n_leaves + 1, FEATURES, CHUNK), BF16),
            pltpu.VMEM((4 * n_leaves + 1, 32, CHUNK), BF16),
            pltpu.VMEM((n_leaves, CHUNK), jnp.int32),
            pltpu.SMEM((n_leaves,), jnp.int32),
            pltpu.SMEM((64,), jnp.int32),
            pltpu.SMEM((40,), jnp.int32),
            *[pltpu.SMEM((len(table), len(table[0])), jnp.int32) for table in tables],
        ],
        flops=us * 10**9,
        seen=us * 10**6,
        name="near_" + phase,
    )(*args)


def per_device(positions, charges, counts, check_to_equiv, up_child, down_child, translate):
    n_points = positions.shape[2]
    n_probe = charges.shape[1]
    n_devices = lax.axis_size(AXES)
    total_bits = n_devices.bit_length() - 1
    shape_of = jax.ShapeDtypeStruct
    half = shape_of((4, ROWS, CHUNK), BF16)
    low, high, shape, equiv = call(
        upward_kernel,
        [SMEM, VMEM, VMEM, VMEM],
        (half, half, shape_of((8, 64, n_points), BF16), shape_of((n_probe, 512), BF16)),
        seen=3 * 10**6,
        flops=3 * 10**9,
        limit=56,
        name="upward",
    )(counts, positions.transpose(1, 0, 2), charges, check_to_equiv)
    move = functools.partial(shifted, total=total_bits)
    z_low = move(high, 2, 1)
    z_high = move(low, 2, -1)
    gathered = lax.all_gather(equiv, AXES, axis=0)
    near, targets, low, high = near_call("first", (low, high), None, counts, None)
    z_low, z_high, near = lax.optimization_barrier((z_low, z_high, near))
    planes = [a.reshape(2, 2, ROWS, CHUNK) for a in (z_low, low, high, z_high)]
    faces = [jnp.stack([a[:, x] for a in planes]).reshape(8, ROWS, CHUNK) for x in range(2)]
    faces[0], faces[1], near = lax.optimization_barrier((faces[0], faces[1], near))
    x_low = move(faces[1], 0, 1)
    x_high = move(faces[0], 0, -1)
    near = near_call("second", (low, high), targets, counts, near)
    x_low, x_high, near = lax.optimization_barrier((x_low, x_high, near))
    plane = shape_of((16, ROWS, CHUNK), BF16)
    y_faces = call(
        faces_kernel, [VMEM] * 6, (plane, plane), seen=3 * 10**6, flops=10**9, name="faces"
    )(x_low, z_low, low, high, z_high, x_high)
    face_0, face_1, near = lax.optimization_barrier((*y_faces, near))
    y_low = move(face_1, 1, 1)
    y_high = move(face_0, 1, -1)
    near = near_call("middle", (z_low, z_high, x_low, x_high), targets, counts, near)
    translate, near = lax.optimization_barrier((translate, near))
    wide = call(
        widen_kernel,
        [VMEM],
        shape_of((7, 7 * 6 * 64, 128), BF16),
        [pltpu.VMEM((3 * CHUNK * 65, 128), F32)],
        limit=56,
        seen=6 * 10**6,
        flops=6 * 10**9,
        name="widen",
    )(translate.transpose(1, 2, 0))
    wide, near, y_low, y_high = lax.optimization_barrier((wide, near, y_low, y_high))
    near = near_call("last", (y_low, y_high), targets, counts, near)
    anywhere = pl.BlockSpec(memory_space=pl.ANY)
    return call(
        functools.partial(far_kernel, total_bits),
        [SMEM, anywhere, anywhere] + [VMEM] * 4,
        shape_of((8, n_probe, n_points), F32),
        [
            pltpu.VMEM((n_devices // 2, 2, n_probe, 512), BF16),
            pltpu.VMEM((7, 7 * 6 * 64, 128), BF16),
            pltpu.VMEM((n_devices // 2, n_probe, 128), BF16),
            pltpu.VMEM((8, n_probe, 36 * 64), BF16),
            pltpu.SemaphoreType.DMA((5,)),
        ],
        seen=10 * 10**6,
        flops=8 * 10**9,
        limit=56,
        name="far",
    )(
        counts,
        gathered.reshape(n_devices // 2, 2, n_probe, 512),
        wide,
        up_child,
        down_child,
        shape,
        near,
    )


def solution(mesh):
    split = P(AXES, None, None)
    return jax.shard_map(
        per_device,
        mesh=mesh,
        in_specs=(split, split, P(AXES), P(), P(), P(), P()),
        out_specs=split,
        check_vma=False,
    )
```

```python
import functools

import jax
import jax.numpy as jnp
from jax import lax
from jax.experimental import pallas as pl
from jax.experimental.pallas import tpu as pltpu
from jax.sharding import PartitionSpec as P

AXES = ("oct", "leaf")
KERNEL_SCALE = 0.02
SOFTENING = 0.01
INVERSE = 1.0 / KERNEL_SCALE**2
CHUNK = 128
ROWS = 144
FEATURES = 48
MIB = 1 << 20
F32 = jnp.float32
BF16 = jnp.bfloat16
VMEM = pl.BlockSpec(memory_space=pltpu.VMEM)
SMEM = pl.BlockSpec(memory_space=pltpu.SMEM)


def bit_counts(total):
    return [(total + 2) // 3, (total + 1) // 3, total // 3]


def box_coords(index, total):
    coords = []
    for j, bits in enumerate(bit_counts(total)):
        value = 0
        for k in range(bits):
            value = value + ((index >> (3 * k + j)) & 1) * 2**k
        coords.append(value)
    return coords


def box_index(coords, total):
    index = 0
    for j, bits in enumerate(bit_counts(total)):
        for k in range(bits):
            index = index + ((coords[j] >> k) & 1) * 2 ** (3 * k + j)
    return index


def shifted(value, axis, step, total):
    pairs = []
    for device in range(2**total):
        coords = box_coords(device, total)
        coords[axis] += step
        if 0 <= coords[axis] < 2 ** bit_counts(total)[axis]:
            pairs.append((device, box_index(coords, total)))
    return lax.ppermute(value, AXES, pairs)


def pieces(x):
    first = x.astype(BF16).astype(F32)
    rest = x - first
    second = rest.astype(BF16).astype(F32)
    third = (rest - second).astype(BF16).astype(F32)
    return first, second, third


def row_index(shape):
    return lax.broadcasted_iota(jnp.int32, shape, 0)


def placed(rows, offsets):
    eight = jnp.concatenate([rows, jnp.zeros_like(rows)], 0)
    index = row_index(eight.shape)
    shift = jnp.where(index == 0, offsets[0], jnp.where(index == 1, offsets[1], offsets[2]))
    return jnp.where(index < 3, eight + shift, 0.0)


def with_rows(base, extra):
    index = row_index(base.shape)
    for k, row in enumerate(extra):
        base = jnp.where(index == 3 + k, row, base)
    return base


def source_features(rows, offsets):
    x = placed(rows, offsets)
    high = x.astype(BF16).astype(F32)
    low = x - high
    norm = INVERSE * jnp.sum(x * x, axis=0, keepdims=True)
    ones = (1.0, 1.0, 1.0)
    groups = [with_rows(high, pieces(norm)), with_rows(high, ones), high, low, low, low]
    return jnp.concatenate(groups, 0)


def target_features(rows, offsets):
    x = placed(rows, offsets)
    w1, w2, w3 = pieces((-2.0 * INVERSE) * x)
    norm = INVERSE * (jnp.sum(x * x, axis=0, keepdims=True) + SOFTENING)
    ones = (1.0, 1.0, 1.0)
    return jnp.concatenate(
        [with_rows(w1, ones), with_rows(w2, pieces(norm)), w3, w1, w2, w3], 0
    )


def upward_kernel(counts, positions, charges, to_equiv, low, high, shape_out, equiv_out):
    n_points = positions.shape[2]
    n_chunks = n_points // CHUNK
    index = lax.broadcasted_iota(jnp.int32, (64, n_points), 0)
    surface = [
        ((index >> (2 * d)) & 3).astype(F32) * 0.5 - 0.25 for d in range(3)
    ]
    slot = lax.broadcasted_iota(jnp.int32, (32, n_points), 1)
    points = [positions[d].astype(F32) for d in range(3)]
    upward = []
    for leaf in range(8):
        out, at = (low, leaf) if leaf < 4 else (high, leaf - 4)
        count = counts[leaf]
        p = [points[d][leaf : leaf + 1] for d in range(3)]
        square = (surface[0] - p[0]) ** 2
        square = square + (surface[1] - p[1]) ** 2
        square = square + (surface[2] - p[2]) ** 2
        shape = (KERNEL_SCALE * lax.rsqrt(square + SOFTENING)).astype(BF16)
        shape_out[leaf] = shape
        q = jnp.where(slot < count, charges[leaf].astype(F32), 0.0).astype(BF16)
        upward.append(
            lax.dot_general(q, shape, (((1,), (1,)), ((), ())), preferred_element_type=F32)
        )
        live = lax.shift_right_logical(count + (CHUNK - 1), 7).astype(F32)
        rows = []
        for j in range(n_chunks):
            at_lanes = slice(CHUNK * j, CHUNK * (j + 1))
            out[at, 32 * j : 32 * j + 32, :] = q[:, at_lanes]
            rows += [row[:, at_lanes] for row in p]
            rows.append(jnp.full((1, CHUNK), live, F32))
        out[at, 128:144, :] = jnp.concatenate(rows, 0).astype(BF16)
    total = jnp.concatenate(upward, 0)
    equiv = jnp.zeros(total.shape, F32)
    for piece in pieces(total)[::-1]:
        equiv = equiv + jnp.dot(piece.astype(BF16), to_equiv[...], preferred_element_type=F32)
    equiv = equiv.astype(BF16)
    equiv_out[...] = jnp.concatenate([equiv[32 * l : 32 * l + 32] for l in range(8)], 1)


def near_kernel(sides, opens, tables, *refs):
    payloads, refs = refs[: len(sides)], refs[len(sides) :]
    if opens:
        counts, out, targets, low, high, *refs = refs
    else:
        targets, before, counts, out, *refs = refs
    features, values, live_v, live_s, queue, aim_queue, leaves, sources, aims = refs
    for table, ref in zip(tables, (leaves, sources, aims)):
        for i, row in enumerate(table):
            for k, entry in enumerate(row):
                ref[i, k] = jnp.int32(entry)
    n_leaves = sum(sides)
    n_tasks, n_sources = sources.shape
    n_aims = aims.shape[1]
    first = 0
    for payload, size in zip(payloads, sides):

        def one(leaf, _, payload=payload, first=first):
            block = payload[leaf, 128:144, :].astype(F32)
            at = first + leaf
            offsets = [leaves[at, d].astype(F32) for d in range(3)]
            for j in range(4):
                features[4 * at + j] = source_features(block[4 * j : 4 * j + 4], offsets).astype(
                    BF16
                )
                values[4 * at + j] = payload[leaf, 32 * j : 32 * j + 32, :]
            live_v[pl.ds(at, 1), :] = block[3:4].astype(jnp.int32)
            return 0

        lax.fori_loop(0, size, one, 0)
        first += size
    features[4 * n_leaves] = features[0]
    values[4 * n_leaves] = jnp.zeros((32, CHUNK), BF16)
    for at in range(n_leaves):
        live_s[at] = live_v[at : at + 1, :][0, 0]
    if opens:
        out[...] = jnp.zeros_like(out)
        low[...] = payloads[0][...]
        high[...] = payloads[1][...]
        for leaf in range(8):
            block = payloads[leaf // 4][leaf % 4, 128:144, :].astype(F32)
            offsets = (leaf % 2 - 1.0, leaf // 2 % 2 - 1.0, leaf // 4 - 1.0)
            for j in range(4):
                rows = target_features(block[4 * j : 4 * j + 4], offsets)
                targets[4 * leaf + j] = rows.T.astype(BF16)
    else:
        out[...] = before[...]

    def compute(start, n_rows, n_items):
        places = [aim_queue[start + i] for i in range(n_rows)]
        rows = jnp.concatenate([targets[place] for place in places], 0)

        def add(at, width, total):
            items = [queue[at + k] for k in range(width)]
            u = jnp.concatenate([features[item] for item in items], 1)
            q = jnp.concatenate([values[item] for item in items], 1)
            square = jnp.dot(rows, u, preferred_element_type=F32)
            kern = lax.rsqrt(square).astype(BF16)
            return total + lax.dot_general(
                q, kern, (((1,), (1,)), ((), ())), preferred_element_type=F32
            )

        def store(total):
            for i, place in enumerate(places):
                out[place] += total[:, CHUNK * i : CHUNK * (i + 1)]

        full = n_items // 12
        rest = n_items - 12 * full
        total = lax.fori_loop(
            0, full, lambda c, t: add(12 * c, 12, t), jnp.zeros((32, CHUNK * n_rows), F32)
        )
        store(total)
        for width in (4, 8, 12):

            @pl.when((rest > width - 4) & (rest <= width))
            def _(width=width):
                store(add(12 * full, width, jnp.zeros((32, CHUNK * n_rows), F32)))

    def task(i, _):
        n_items = jnp.int32(0)
        for k in range(n_sources):
            leaf = sources[i, k]
            n_live = jnp.where(leaf >= 0, live_s[jnp.maximum(leaf, 0)], 0)
            for j in range(4):
                queue[n_items] = 4 * leaf + j
                n_items = n_items + (j < n_live).astype(jnp.int32)
        for k in range(12):
            queue[n_items + k] = 4 * n_leaves
        n_rows = jnp.int32(0)
        for k in range(n_aims):
            leaf = aims[i, k]
            count = jnp.where(leaf >= 0, counts[jnp.maximum(leaf, 0)], 0)
            for j in range(4):
                aim_queue[n_rows] = 4 * leaf + j
                n_rows = n_rows + (CHUNK * j < count).astype(jnp.int32)

        @pl.when(n_items > 0)
        def _():
            full = n_rows // 4

            def four(c, _):
                compute(4 * c, 4, n_items)
                return 0

            lax.fori_loop(0, full, four, 0)
            for rest in (1, 2, 3):

                @pl.when(n_rows - 4 * full == rest)
                def _(rest=rest):
                    compute(4 * full, rest, n_items)

        return 0

    lax.fori_loop(0, n_tasks, task, 0)


def faces_kernel(x_low, z_low, low, high, z_high, x_high, *faces):
    for y in range(2):
        for z, plane in enumerate((z_low, low, high, z_high)):
            faces[y][4 * z] = x_low[2 * z + y]
            faces[y][4 * z + 1] = plane[2 * y]
            faces[y][4 * z + 2] = plane[2 * y + 1]
            faces[y][4 * z + 3] = x_high[2 * z + y]


def widen_kernel(table, wide, rows):
    n_equiv = table.shape[0]
    window = 6 * n_equiv
    n_offsets = table.shape[2]
    n_lanes = 3 * CHUNK
    stride = n_equiv + 1
    together = 16
    unit = row_index((CHUNK, CHUNK)) == lax.broadcasted_iota(jnp.int32, (CHUNK, CHUNK), 1)
    unit = jnp.where(unit, 1.0, 0.0).astype(BF16)

    def turn(i, _):
        parts = []
        for m in range(together):
            x = jnp.concatenate(
                [
                    table[together * i + m].astype(F32),
                    jnp.zeros((n_equiv, n_lanes - n_offsets), F32),
                ],
                1,
            )
            parts += [pltpu.roll(x, n_lanes - 1, 1), x]
        both = jnp.concatenate(parts, 0).astype(BF16)
        for c in range(n_lanes // CHUNK):
            turned = lax.dot_general(
                unit,
                both[:, CHUNK * c : CHUNK * (c + 1)],
                (((1,), (1,)), ((), ())),
                preferred_element_type=F32,
            )
            for m in range(together):
                at = pl.ds(CHUNK * c * stride + together * i + m, CHUNK, stride=stride)
                rows[at, :] = turned[:, CHUNK * m : CHUNK * (m + 1)]
        return 0

    lax.fori_loop(0, n_equiv // together, turn, 0)
    index = lax.broadcasted_iota(jnp.int32, (window, 2 * n_equiv), 0)
    lane = lax.broadcasted_iota(jnp.int32, (window, 2 * n_equiv), 1)
    first = jnp.where(lane < n_equiv, n_equiv, 2 * n_equiv)
    beside = (index >= first) & (index < first + 3 * n_equiv)

    def pack(i, _):
        oz, oy = i // 7, i % 7
        near = (jnp.abs(oz - 3) <= 1) & (jnp.abs(oy - 3) <= 1)
        block = jnp.concatenate(
            [rows[pl.ds((7 * i + x) * stride, n_equiv), :] for x in range(6)], 0
        )
        block = jnp.where(near & beside, 0.0, block)
        wide[oz, pl.ds(pl.multiple_of(oy * window, window), window), :] = block.astype(BF16)
        return 0

    lax.fori_loop(0, 49, pack, 0)


def far_kernel(
    total_bits,
    counts,
    gathered_hbm,
    wide_hbm,
    up,
    down,
    shape,
    near,
    out,
    gathered,
    wide,
    boxes,
    region,
    sems,
):
    n_equiv = 64
    window = 6 * n_equiv
    bits = bit_counts(total_bits)
    n_pairs = gathered.shape[0]
    step = n_pairs // 4
    copies = []
    for i in range(4):
        part = pl.ds(step * i, step)
        copies.append(pltpu.make_async_copy(gathered_hbm.at[part], gathered.at[part], sems.at[i]))
    copies.append(pltpu.make_async_copy(wide_hbm, wide, sems.at[4]))
    for copy in copies:
        copy.start()
    me = lax.axis_index("oct") * lax.axis_size("leaf") + lax.axis_index("leaf")
    cx, cy, cz = box_coords(me, total_bits)
    zeros_up = jnp.zeros((8 * n_equiv, n_equiv), F32)
    up_rows = up[...].astype(F32).reshape(8 * n_equiv, n_equiv)
    up_even = jnp.concatenate([up_rows, zeros_up], 1).astype(BF16)
    up_odd = jnp.concatenate([zeros_up, up_rows], 1).astype(BF16)
    for i in range(4):
        copies[i].wait()
        at = slice(step * i, step * (i + 1))
        even = gathered[at, 0].reshape(step * 32, 8 * n_equiv)
        odd = gathered[at, 1].reshape(step * 32, 8 * n_equiv)
        both = jnp.dot(even, up_even, preferred_element_type=F32)
        both = both + jnp.dot(odd, up_odd, preferred_element_type=F32)
        boxes[at] = both.astype(BF16).reshape(step, 32, 2 * n_equiv)

    region[0] = jnp.zeros_like(region[0])
    region[7] = jnp.zeros_like(region[7])
    for bz in range(3):
        for by in range(3):
            for bx in range(3):
                z, y, x = cz + bz - 1, cy + by - 1, cx + bx - 1
                inside = (
                    (z >= 0)
                    & (z < 2 ** bits[2])
                    & (y >= 0)
                    & (y < 2 ** bits[1])
                    & (x >= 0)
                    & (x < 2 ** bits[0])
                )
                box = jnp.where(inside, box_index([x, y, z], total_bits), 0)
                data = gathered[box >> 1, box & 1]
                data = jnp.where(inside, data, jnp.zeros_like(data))
                for lz in range(2):
                    for ly in range(2):
                        at = (2 * by + ly) * window + bx * 2 * n_equiv
                        part = (2 * lz + ly) * 2 * n_equiv
                        region[1 + 2 * bz + lz, :, at : at + 2 * n_equiv] = data[
                            :, part : part + 2 * n_equiv
                        ]

    copies[4].wait()

    parent = cx >> 1
    total = jnp.zeros((32, 2 * n_equiv), F32)
    zero = jnp.zeros((32, 2 * n_equiv), BF16)
    span_y = 2 ** bits[1]
    for z in range(2 ** bits[2]):
        row = []
        for y in range(span_y):
            for dx in (-1, 0, 1):
                px = parent + dx
                inside = (px >= 0) & (px < 2 ** (bits[0] - 1))
                pair = box_index([2 * jnp.where(inside, px, 0), y, z], total_bits) >> 1
                row.append(jnp.where(inside, boxes[pair], zero))
        start = pl.multiple_of((3 - cy) * window, window)
        right = wide[z - cz + 3, pl.ds(start, span_y * window), :]
        total = total + jnp.dot(jnp.concatenate(row, 1), right, preferred_element_type=F32)
    total = jnp.where((cx & 1) == 0, total, pltpu.roll(total, n_equiv, 1))
    box_local = (0.5 * total[:, :n_equiv]).astype(BF16)
    down_row = jnp.concatenate([down[l] for l in range(8)], 1)
    inherited = jnp.dot(box_local, down_row, preferred_element_type=F32)

    sums = [jnp.zeros((64, 2 * n_equiv), F32) for _ in range(2)]
    for a in range(7):
        left = region[a : a + 2].reshape(64, 6 * window)
        for ty in range(2):
            right = wide[a, (1 - ty) * window : (7 - ty) * window, :]
            sums[ty] = sums[ty] + jnp.dot(left, right, preferred_element_type=F32)
    n_points = out.shape[2]
    slot = lax.broadcasted_iota(jnp.int32, (32, n_points), 1)
    lane = lax.broadcasted_iota(jnp.int32, (32, 2 * n_equiv), 1)
    for tz in range(2):
        for ty in range(2):
            first = 4 * tz + 2 * ty
            local = (
                inherited[:, first * n_equiv : (first + 2) * n_equiv]
                + sums[ty][32 * tz : 32 * tz + 32]
            )
            left = jnp.concatenate(
                [jnp.where(lane < n_equiv, local, 0.0), jnp.where(lane < n_equiv, 0.0, local)], 0
            ).astype(BF16)
            right = shape[first : first + 2].reshape(2 * n_equiv, n_points)
            far = jnp.dot(left, right, preferred_element_type=F32)
            for tx in range(2):
                value = jnp.concatenate([near[4 * (first + tx) + j] for j in range(4)], 1)
                value = value + far[32 * tx : 32 * tx + 32]
                out[first + tx] = jnp.where(slot < counts[first + tx], value, 0.0)


def call(kernel, ins, outs, scratch=(), flops=0, seen=0, limit=28, **kwargs):
    return pl.pallas_call(
        kernel,
        out_shape=outs,
        in_specs=ins,
        out_specs=jax.tree.map(lambda _: VMEM, outs),
        scratch_shapes=list(scratch),
        compiler_params=pltpu.CompilerParams(vmem_limit_bytes=limit * MIB),
        cost_estimate=pl.CostEstimate(flops=flops, bytes_accessed=seen, transcendentals=0),
        **kwargs,
    )


def near_tables():
    both = range(2)
    own = [(x, y, z) for z in (1, 2) for y in (1, 2) for x in (1, 2)]
    z_side = [(x, y, 3 * side) for side in both for y in (1, 2) for x in (1, 2)]
    x_side = [(3 * side, y, z) for side in both for z in range(4) for y in (1, 2)]
    y_side = [(x, 3 * side, z) for side in both for z in range(4) for x in range(4)]
    eight = list(range(8))
    middle = []
    for side in both:
        four = [4 * side + i for i in range(4)]
        middle.append((four, four))
    for tx in both:
        for tz in both:
            six = [8 + 8 * tx + 2 * tz + i for i in range(6)]
            middle.append((six, [4 * tz + 2 * ty + tx for ty in both]))
    last = []
    for ty in both:
        for tz in both:
            for tx in both:
                nine = [
                    16 * ty + 4 * (tz + dz) + tx + dx for dz in range(3) for dx in range(3)
                ]
                last.append((nine, [4 * tz + 2 * ty + tx]))
    return {
        "first": ((4, 4), own, [(eight, [0, 1, 2, 3])]),
        "second": ((4, 4), own, [(eight, [4, 5, 6, 7])]),
        "middle": ((4, 4, 8, 8), z_side + x_side, middle),
        "last": ((16, 16), y_side, last),
    }


def near_call(phase, payloads, targets, counts, before):
    sides, places, tasks = near_tables()[phase]
    n_leaves = sum(sides)
    n_sources = max(len(task[0]) for task in tasks)
    n_aims = max(len(task[1]) for task in tasks)
    pad = lambda row, size: row + [-1] * (size - len(row))
    tables = [
        [[c - 2 for c in place] for place in places],
        [pad(task[0], n_sources) for task in tasks],
        [pad(task[1], n_aims) for task in tasks],
    ]
    opens = before is None
    args = list(payloads)
    outs = jax.ShapeDtypeStruct((32, 32, CHUNK), F32)
    if opens:
        half = jax.ShapeDtypeStruct(payloads[0].shape, BF16)
        outs = (outs, jax.ShapeDtypeStruct((32, CHUNK, FEATURES), BF16), half, half)
    else:
        args += [targets, before]
    args.append(counts)
    us = {"first": 12, "second": 12, "middle": 25, "last": 15}[phase]
    return call(
        functools.partial(near_kernel, sides, opens, tables),
        [VMEM] * (len(args) - 1) + [SMEM],
        outs,
        [
            pltpu.VMEM((4 * n_leaves + 1, FEATURES, CHUNK), BF16),
            pltpu.VMEM((4 * n_leaves + 1, 32, CHUNK), BF16),
            pltpu.VMEM((n_leaves, CHUNK), jnp.int32),
            pltpu.SMEM((n_leaves,), jnp.int32),
            pltpu.SMEM((64,), jnp.int32),
            pltpu.SMEM((40,), jnp.int32),
            *[pltpu.SMEM((len(table), len(table[0])), jnp.int32) for table in tables],
        ],
        flops=us * 10**9,
        seen=us * 10**6,
        name="near_" + phase,
    )(*args)


def per_device(positions, charges, counts, check_to_equiv, up_child, down_child, translate):
    n_points = positions.shape[2]
    n_probe = charges.shape[1]
    n_devices = lax.axis_size(AXES)
    total_bits = n_devices.bit_length() - 1
    shape_of = jax.ShapeDtypeStruct
    half = shape_of((4, ROWS, CHUNK), BF16)
    low, high, shape, equiv = call(
        upward_kernel,
        [SMEM, VMEM, VMEM, VMEM],
        (half, half, shape_of((8, 64, n_points), BF16), shape_of((n_probe, 512), BF16)),
        seen=3 * 10**6,
        flops=3 * 10**9,
        limit=56,
        name="upward",
    )(counts, positions.transpose(1, 0, 2), charges, check_to_equiv)
    move = functools.partial(shifted, total=total_bits)
    z_low = move(high, 2, 1)
    z_high = move(low, 2, -1)
    gathered = lax.all_gather(equiv, AXES, axis=0)
    near, targets, low, high = near_call("first", (low, high), None, counts, None)
    z_low, z_high, near = lax.optimization_barrier((z_low, z_high, near))
    planes = [a.reshape(2, 2, ROWS, CHUNK) for a in (z_low, low, high, z_high)]
    faces = [jnp.stack([a[:, x] for a in planes]).reshape(8, ROWS, CHUNK) for x in range(2)]
    faces[0], faces[1], near = lax.optimization_barrier((faces[0], faces[1], near))
    x_low = move(faces[1], 0, 1)
    x_high = move(faces[0], 0, -1)
    near = near_call("second", (low, high), targets, counts, near)
    x_low, x_high, near = lax.optimization_barrier((x_low, x_high, near))
    plane = shape_of((16, ROWS, CHUNK), BF16)
    y_faces = call(
        faces_kernel, [VMEM] * 6, (plane, plane), seen=3 * 10**6, flops=10**9, name="faces"
    )(x_low, z_low, low, high, z_high, x_high)
    face_0, face_1, near = lax.optimization_barrier((*y_faces, near))
    y_low = move(face_1, 1, 1)
    y_high = move(face_0, 1, -1)
    near = near_call("middle", (z_low, z_high, x_low, x_high), targets, counts, near)
    translate, near = lax.optimization_barrier((translate, near))
    wide = call(
        widen_kernel,
        [VMEM],
        shape_of((7, 7 * 6 * 64, 128), BF16),
        [pltpu.VMEM((3 * CHUNK * 65 + CHUNK, 128), F32)],
        limit=56,
        seen=6 * 10**6,
        flops=6 * 10**9,
        name="widen",
    )(translate.transpose(1, 2, 0))
    wide, near, y_low, y_high = lax.optimization_barrier((wide, near, y_low, y_high))
    near = near_call("last", (y_low, y_high), targets, counts, near)
    anywhere = pl.BlockSpec(memory_space=pl.ANY)
    return call(
        functools.partial(far_kernel, total_bits),
        [SMEM, anywhere, anywhere] + [VMEM] * 4,
        shape_of((8, n_probe, n_points), F32),
        [
            pltpu.VMEM((n_devices // 2, 2, n_probe, 512), BF16),
            pltpu.VMEM((7, 7 * 6 * 64, 128), BF16),
            pltpu.VMEM((n_devices // 2, n_probe, 128), BF16),
            pltpu.VMEM((8, n_probe, 36 * 64), BF16),
            pltpu.SemaphoreType.DMA((5,)),
        ],
        seen=10 * 10**6,
        flops=8 * 10**9,
        limit=56,
        name="far",
    )(
        counts,
        gathered.reshape(n_devices // 2, 2, n_probe, 512),
        wide,
        up_child,
        down_child,
        shape,
        near,
    )


def solution(mesh):
    split = P(AXES, None, None)
    return jax.shard_map(
        per_device,
        mesh=mesh,
        in_specs=(split, split, P(AXES), P(), P(), P(), P()),
        out_specs=split,
        check_vma=False,
    )
```
